32 devices in a mesh: replica: 4 (over x, core), fsdp: 8 (over z, y).
Axes of the slice: x: 2, y: 2, z: 4, core: 2. Of those that a mesh axis runs over, the one named last changes fastest.
Arguments:
- tokens: bfloat16 [8192, 2048], P(('replica', 'fsdp')), may hold values from -6 to 6
- seq_lengths: int32 [32, 2], P(('replica', 'fsdp')), may hold values from 0 to 256, as said below
- attn_gain: bfloat16 [2048], P('fsdp'), may hold values from 0.099609375 to 1.8984375
- w_query: bfloat16 [2048, 2048], P('fsdp'), may hold values from -0.125 to 0.125
- w_key: bfloat16 [2048, 2048], P('fsdp'), may hold values from -0.125 to 0.125
- w_value: bfloat16 [2048, 2048], P('fsdp'), may hold values from -0.125 to 0.125
- w_outgate: bfloat16 [2048, 2048], P('fsdp'), may hold values from -0.125 to 0.125
- w_alpha: bfloat16 [2048, 16], P('fsdp'), may hold values from -0.125 to 0.125
- w_beta: bfloat16 [2048, 16], P('fsdp'), may hold values from -0.125 to 0.125
- conv_weight: bfloat16 [4, 6144], P(None, 'fsdp'), may hold values from -3 to 3
- decay_log: float32 [16], replicated, may hold values from -1.5 to 1.5
- decay_bias: float32 [16], replicated, may hold values from -7 to -2
- head_gain: float32 [128], replicated, may hold values from 0.1 to 1.9
- w_output: bfloat16 [2048, 2048], P('fsdp'), may hold values from -0.125 to 0.125
- mlp_gain: bfloat16 [2048], P('fsdp'), may hold values from 0.099609375 to 1.8984375
- w_gate: bfloat16 [2048, 5632], P('fsdp'), may hold values from -0.125 to 0.125
- w_up: bfloat16 [2048, 5632], P('fsdp'), may hold values from -0.125 to 0.125
- w_down: bfloat16 [5632, 2048], P('fsdp'), may hold values from -0.078125 to 0.078125
- cotangent: bfloat16 [8192, 2048], P(('replica', 'fsdp')), may hold values from -6 to 6
Outputs:
- output: bfloat16 [8192, 2048], P(('replica', 'fsdp'))
- grad_tokens: bfloat16 [8192, 2048], P(('replica', 'fsdp'))
- grad_attn_gain: float32 [2048], P('fsdp')
- grad_query: float32 [2048, 2048], P('fsdp')
- grad_key: float32 [2048, 2048], P('fsdp')
- grad_value: float32 [2048, 2048], P('fsdp')
- grad_outgate: float32 [2048, 2048], P('fsdp')
- grad_alpha: float32 [2048, 16], P('fsdp')
- grad_beta: float32 [2048, 16], P('fsdp')
- grad_conv: float32 [4, 6144], P(None, 'fsdp')
- grad_decay_log: float32 [16], replicated
- grad_decay_bias: float32 [16], replicated
- grad_head_gain: float32 [128], replicated
- grad_output_proj: float32 [2048, 2048], P('fsdp')
- grad_mlp_gain: float32 [2048], P('fsdp')
- grad_gate: float32 [2048, 5632], P('fsdp')
- grad_up: float32 [2048, 5632], P('fsdp')
- grad_down: float32 [5632, 2048], P('fsdp')
The draws below stay inside these ranges and needn't reach their ends.
Inputs may be any that keep to these rules, and one draw needn't show every extreme that they name: `seq_lengths`: row r describes buffer r: its sequences are packed in order from row 0 of the buffer, the first of length 64 or more; every length is a multiple of 64 and a row sums to at most 256; rows after that sum are padding. In every draw some buffer holds one sequence of 256 rows and some other buffer is filled to 256.
All inputs are finite; a program needn't handle non-finite values.
Results may differ from the reference program's by a relative error of at most 0.019.
Values may be sent and summed in bfloat16 or wider, within the bound.
No kernel may reach another device: no remote copies, remote signals or barrier semaphores. Data moves between devices by JAX's collectives and lax.ppermute only.
A program may use at most 512 MiB of HBM per device.

```python
import jax
import jax.numpy as jnp
from jax import lax

D = 2048
HEADS = 16
HEAD = 128
FF = 5632
CONV = 4
BLOCK = 64
CAP = 256
BUFFERS = 32
TOKENS = 8192


def draw_seq_lengths(key, part):
    key = jax.random.fold_in(key, 11)
    first_key, second_key, pick_key = jax.random.split(key, 3)
    blocks_all = CAP // BLOCK
    row_ids = jnp.arange(BUFFERS, dtype=jnp.int32)
    chosen = jax.random.permutation(pick_key, BUFFERS).astype(jnp.int32)
    first_len = jax.random.randint(first_key, (BUFFERS,), 1, blocks_all + 1)
    first_len = jnp.where(row_ids == chosen[1], blocks_all, first_len)
    remain = blocks_all - first_len
    second = jax.random.randint(second_key, (BUFFERS,), 0, remain + 1)
    second = jnp.where(row_ids == chosen[0], remain, second)
    return (jnp.stack([first_len, second], axis=1) * BLOCK).astype(jnp.int32)


def block_levels(rng, dims, cuts, smallest, high):
    factor_of = 1.0
    for axis_at, blocks in cuts:
        draws = jax.random.uniform(jax.random.fold_in(jax.random.fold_in(rng, 6), axis_at), (blocks,), jnp.float32, smallest / len(cuts), high / len(cuts))
        factor_of = factor_of * jnp.repeat(jnp.exp(draws), dims[axis_at] // blocks).reshape((-1,) + (1,) * (len(dims) - 1 - axis_at))
    return factor_of


def centred(stream_key, dims, scale, bound, cuts=(), kind=jnp.bfloat16):
    level = block_levels(stream_key, dims, cuts, -0.22, 0.18) if cuts else 1.0
    result = jax.random.normal(stream_key, dims, jnp.float32) * scale * level
    return jnp.minimum(jnp.maximum(result, -bound), bound).astype(kind)


def setup_inputs(seed: int = 0) -> dict:
    key_of = jax.random.split(jax.random.key(seed), 20)
    tokens = centred(key_of[0], (TOKENS, D), 1.0, 6.0, ((0, 32),))
    seq_lengths = draw_seq_lengths(jax.random.fold_in(key_of[19], 71), 0)
    attn_gain = jnp.clip(1.0 + 0.18 * jax.random.normal(key_of[2], (D,), jnp.float32), 0.099609375, 1.8984375).astype(jnp.bfloat16)
    w_query = centred(key_of[3], (D, D), D ** -0.5, 0.125, ((0, 8),))
    w_key = centred(key_of[4], (D, D), D ** -0.5, 0.125, ((0, 8),))
    w_value = centred(key_of[5], (D, D), D ** -0.5, 0.125, ((0, 8),))
    w_outgate = centred(key_of[6], (D, D), D ** -0.5, 0.125, ((0, 8),))
    w_alpha = centred(key_of[7], (D, HEADS), D ** -0.5, 0.125, ((0, 8),))
    w_beta = centred(key_of[8], (D, HEADS), D ** -0.5, 0.125, ((0, 8),))
    conv_weight = centred(key_of[9], (CONV, 3 * D), CONV ** -0.5, 3.0, ((1, 8),))
    decay_log = jnp.clip(jax.random.uniform(key_of[10], (HEADS,), jnp.float32, -1.5, 1.5), -1.5, 1.5)
    decay_bias = jnp.clip(jax.random.uniform(key_of[11], (HEADS,), jnp.float32, -7.0, -2.0), -7.0, -2.0)
    head_gain = jnp.clip(1.0 + 0.18 * jax.random.normal(key_of[12], (HEAD,), jnp.float32), 0.1, 1.9)
    w_output = centred(key_of[13], (D, D), D ** -0.5, 0.125, ((0, 8),))
    mlp_gain = jnp.clip(1.0 + 0.18 * jax.random.normal(key_of[14], (D,), jnp.float32), 0.099609375, 1.8984375).astype(jnp.bfloat16)
    w_gate = centred(key_of[15], (D, FF), D ** -0.5, 0.125, ((0, 8),))
    w_up = centred(key_of[16], (D, FF), D ** -0.5, 0.125, ((0, 8),))
    w_down = centred(key_of[17], (FF, D), FF ** -0.5, 0.078125, ((0, 8),))
    cotangent = centred(key_of[18], (TOKENS, D), 1.0, 6.0, ((0, 32),))
    return {"tokens": tokens, "seq_lengths": seq_lengths, "attn_gain": attn_gain, "w_query": w_query, "w_key": w_key, "w_value": w_value, "w_outgate": w_outgate, "w_alpha": w_alpha, "w_beta": w_beta, "conv_weight": conv_weight, "decay_log": decay_log, "decay_bias": decay_bias, "head_gain": head_gain, "w_output": w_output, "mlp_gain": mlp_gain, "w_gate": w_gate, "w_up": w_up, "w_down": w_down, "cotangent": cotangent}


EPS = 1e-06

@jax.custom_vjp
def low(v):
    return lax.optimization_barrier(v.astype(jnp.bfloat16)).astype(jnp.float32)

@jax.custom_vjp
def low_back(v):
    return v

def low_keep(v):
    return (low(v), None)

def low_pass(kept, grad):
    return (grad,)

def back_keep(v):
    return (v, None)

def back_low(kept, grad):
    return (low(grad),)
low.defvjp(low_keep, low_pass)
low_back.defvjp(back_keep, back_low)

def exact_dot(left, right):
    return jnp.dot(left, right, precision=lax.Precision.HIGHEST, preferred_element_type=jnp.float32)

def rms_scale(values, gain):
    return values * lax.rsqrt(lax.optimization_barrier(jnp.mean(values * values, axis=-1, keepdims=True)) + EPS) * gain

def segment_layout(lengths, cap_rows, block_rows):
    bounds = jnp.cumsum(lengths).astype(jnp.int32)
    places = jnp.arange(cap_rows, dtype=jnp.int32)
    below = bounds[None, :] <= places[:, None]
    seg_start = lax.optimization_barrier(jnp.max(jnp.where(below, bounds[None, :], 0), axis=1)).astype(jnp.int32)
    offset = places - seg_start
    live_rows = (places < bounds[-1]).astype(jnp.float32)
    firsts = jnp.arange(cap_rows // block_rows, dtype=jnp.int32) * block_rows
    begins = jnp.any(firsts[:, None] == bounds[None, :], axis=1) | (firsts == 0)
    return (offset, begins.astype(jnp.float32), live_rows)

def short_conv(pre_rows, taps, offset):
    summed = pre_rows * taps[0]
    for shift_by in range(1, taps.shape[0]):
        moved = jnp.concatenate([jnp.zeros((shift_by, pre_rows.shape[1]), pre_rows.dtype), pre_rows[:-shift_by]], axis=0)
        summed = summed + jnp.where((offset >= shift_by)[:, None], moved, 0.0) * taps[shift_by]
    return jax.nn.silu(summed)

def unit_heads(values, head_count):
    pieces = values.reshape(values.shape[0], head_count, -1)
    return pieces * lax.rsqrt(lax.optimization_barrier(jnp.sum(pieces * pieces, axis=-1, keepdims=True)) + EPS)

def block_step(carried_state, inputs):
    query_rows_in, key_rows, value_rows, decay, beta, begins = inputs
    accurate_product = lax.Precision.HIGHEST
    carried_state = carried_state * (1.0 - begins)
    size = decay.shape[-1]
    running = jnp.cumsum(decay, axis=-1)
    places = jnp.arange(size)
    strict = places[:, None] > places[None, :]
    within = places[:, None] >= places[None, :]
    spread = running[:, :, None] - running[:, None, :]
    fall_strict = jnp.where(strict, jnp.exp(jnp.where(strict, spread, 0.0)), 0.0)
    fall_within = jnp.where(within, jnp.exp(jnp.where(within, spread, 0.0)), 0.0)
    keys_keys = jnp.einsum('hik,hjk->hij', key_rows, key_rows, precision=accurate_product)
    lower = beta[:, :, None] * fall_strict * keys_keys
    inverse = jnp.eye(size, dtype=lower.dtype) - lower
    power = lower
    reach = 2
    while reach < size:
        power = jnp.einsum('hij,hjk->hik', power, power, precision=accurate_product)
        inverse = inverse + jnp.einsum('hij,hjk->hik', inverse, power, precision=accurate_product)
        reach = reach * 2
    boost_factor = jnp.exp(running)
    corrected_weights = jnp.einsum('hij,hjk->hik', inverse, (beta * boost_factor)[:, :, None] * key_rows, precision=accurate_product)
    corrected_values = jnp.einsum('hij,hjk->hik', inverse, beta[:, :, None] * value_rows, precision=accurate_product)
    update_term = corrected_values - jnp.einsum('fla,fas->fls', corrected_weights, carried_state, precision=accurate_product)
    scores = jnp.einsum('hik,hjk->hij', query_rows_in, key_rows, precision=accurate_product) * fall_within
    outcome_value = jnp.einsum('fla,fas->fls', query_rows_in * boost_factor[:, :, None], carried_state, precision=accurate_product)
    outcome_value = outcome_value + jnp.einsum('hij,hjv->hiv', scores, update_term, precision=accurate_product)
    final_cumulative = running[:, -1]
    decayed_state = key_rows * jnp.exp(final_cumulative[:, None] - running)[:, :, None]
    updated_state = jnp.exp(final_cumulative)[:, None, None] * carried_state + jnp.einsum('zad,zar->zdr', decayed_state, update_term, precision=accurate_product)
    return (updated_state, outcome_value)

def to_blocks(values, block_count):
    shaped = values.reshape((block_count, values.shape[0] // block_count) + values.shape[1:])
    return jnp.swapaxes(shaped, 1, 2)

def delta_rule(query_rows_in, key_rows, value_rows, decay, beta, block_starts):
    block_count = block_starts.shape[0]
    length, head_count, head_size = query_rows_in.shape
    initial = jnp.zeros((head_count, head_size, value_rows.shape[2]), jnp.float32)
    scanned = (to_blocks(query_rows_in, block_count), to_blocks(key_rows, block_count), to_blocks(value_rows, block_count), to_blocks(decay, block_count), to_blocks(beta, block_count), block_starts)
    final_state, results = lax.scan(jax.checkpoint(block_step), initial, scanned)
    return jnp.swapaxes(results, 1, 2).reshape(length, head_count, value_rows.shape[2])

def mixer_inputs(query_pre, key_pre, value_pre, conv_f, offset, head_count):
    width = query_pre.shape[1]
    head_size = width // head_count
    conv_q = short_conv(query_pre, conv_f[:, :width], offset)
    conv_k = short_conv(key_pre, conv_f[:, width:2 * width], offset)
    conv_v = short_conv(value_pre, conv_f[:, 2 * width:], offset)
    query_rows_in = unit_heads(conv_q, head_count) * head_size ** (-0.5)
    key_rows = unit_heads(conv_k, head_count)
    value_rows = conv_v.reshape(query_pre.shape[0], head_count, head_size)
    return (query_rows_in, key_rows, value_rows)

def mixer_core(query_rows_in, key_rows, value_rows, gate_pre, alpha_pre, beta_pre, decay_log, decay_bias, head_gain, block_starts):
    decay = -jnp.exp(decay_log) * jax.nn.softplus(alpha_pre + decay_bias)
    beta = jax.nn.sigmoid(beta_pre)
    mixed = delta_rule(query_rows_in, key_rows, value_rows, decay, beta, block_starts)
    normed = mixed * lax.rsqrt(lax.optimization_barrier(jnp.mean(mixed * mixed, axis=-1, keepdims=True)) + EPS) * head_gain
    gated = normed * jax.nn.silu(gate_pre.reshape(mixed.shape))
    return gated.reshape(gate_pre.shape)

def layer(rows_in, attn_gain, w_query, w_key, w_value, w_outgate, w_alpha, w_beta, conv_weight, decay_log, decay_bias, head_gain, w_output, mlp_gain, w_gate, w_up, w_down, offset, block_starts, live_rows):
    head_count = decay_log.shape[0]
    normed = low(rms_scale(rows_in, attn_gain))
    query_pre = low_back(exact_dot(normed, w_query))
    key_pre = low_back(exact_dot(normed, w_key))
    value_pre = low_back(exact_dot(normed, w_value))
    gate_pre = low_back(exact_dot(normed, w_outgate))
    alpha_pre = low_back(exact_dot(normed, w_alpha))
    beta_pre = low_back(exact_dot(normed, w_beta))
    query_rows_in, key_rows, value_rows = mixer_inputs(query_pre, key_pre, value_pre, conv_weight, offset, head_count)
    query_rows_in = low_back(low(query_rows_in))
    key_rows = low_back(low(key_rows))
    value_rows = low_back(low(value_rows))
    gated = low(mixer_core(query_rows_in, key_rows, value_rows, gate_pre, alpha_pre, beta_pre, decay_log, decay_bias, head_gain, block_starts))
    branch = low_back(exact_dot(gated, w_output))
    resid = rows_in + branch
    normed_two = low(rms_scale(resid, mlp_gain))
    gate_rows = low_back(exact_dot(normed_two, w_gate))
    up_rows = low_back(exact_dot(normed_two, w_up))
    hidden = low(jax.nn.silu(gate_rows) * up_rows)
    return (resid + exact_dot(hidden, w_down)) * live_rows[:, None]

def reference(tokens, seq_lengths, attn_gain, w_query, w_key, w_value, w_outgate, w_alpha, w_beta, conv_weight, decay_log, decay_bias, head_gain, w_output, mlp_gain, w_gate, w_up, w_down, cotangent):
    params = tuple((item.astype(jnp.float32) for item in (attn_gain, w_query, w_key, w_value, w_outgate, w_alpha, w_beta, conv_weight, decay_log, decay_bias, head_gain, w_output, mlp_gain, w_gate, w_up, w_down)))
    token_rows = tokens.astype(jnp.float32).reshape(BUFFERS, CAP, D)
    cot_rows = cotangent.astype(jnp.float32).reshape(BUFFERS, CAP, D)

    def visit(totals, entry):
        rows_here, cot_here, lengths = entry
        offset, block_starts, live_rows = segment_layout(lengths, CAP, BLOCK)

        def run(rows_in, *weights):
            return layer(rows_in, *weights, offset, block_starts, live_rows)
        outcome_value, pullback = jax.vjp(run, rows_here, *params)
        grads = pullback(cot_here)
        totals = tuple((total + grad for total, grad in zip(totals, grads[1:])))
        return (totals, (outcome_value, grads[0]))
    zeros_all = tuple((jnp.zeros_like(item) for item in params))
    totals, (results, back_rows) = lax.scan(visit, zeros_all, (token_rows, cot_rows, seq_lengths))
    g_attn_gain, g_query, g_key, g_value, g_outgate, g_alpha, g_beta, g_conv, g_decay_log, g_decay_bias, g_head_gain, g_output, g_mlp_gain, g_gate, g_up, g_down = totals
    output = results.reshape(TOKENS, D).astype(jnp.bfloat16)
    grad_tokens = back_rows.reshape(TOKENS, D).astype(jnp.bfloat16)
    return (output, grad_tokens, g_attn_gain, g_query, g_key, g_value, g_outgate, g_alpha, g_beta, g_conv, g_decay_log, g_decay_bias, g_head_gain, g_output, g_mlp_gain, g_gate, g_up, g_down)
```

```python
from functools import partial
import jax, jax.numpy as jnp
from jax import lax
from jax.experimental import pallas as pl
from jax.experimental.pallas import tpu as pltpu
from jax.sharding import PartitionSpec as P

EPS = 1e-06
BF = jnp.bfloat16
F32 = jnp.float32
NN = (((1,), (0,)), ((), ()))
NT = (((1,), (1,)), ((), ()))
TN = (((0,), (0,)), ((), ()))


def one_pass(left, right, dims=NN):
    return lax.dot_general(left.astype(BF), right.astype(BF), dims, preferred_element_type=F32)


def halves(value):
    high = value.astype(BF)
    return high, (value - high.astype(F32)).astype(BF)


def three_pass(left, right, dims=NN):
    lh, ll = left if isinstance(left, tuple) else halves(left)
    rh, rl = right if isinstance(right, tuple) else halves(right)
    total = lax.dot_general(lh, rh, dims, preferred_element_type=F32)
    total = total + lax.dot_general(lh, rl, dims, preferred_element_type=F32)
    return total + lax.dot_general(ll, rh, dims, preferred_element_type=F32)


def layout(length_of, count, rows):
    col = lax.broadcasted_iota(jnp.int32, (rows, 1), 0)
    row = lax.broadcasted_iota(jnp.int32, (1, rows), 1)
    bound = jnp.int32(0)
    start_col = jnp.zeros_like(col)
    start_row = jnp.zeros_like(row)
    for at in range(count):
        bound = bound + length_of(at)
        start_col = jnp.where(col >= bound, bound, start_col)
        start_row = jnp.where(row >= bound, bound, start_row)
    same = start_col == start_row
    within = same & (col >= row)
    strict = same & (col > row)
    return col, row, col - start_col, within, strict


def conv_sum(pre, taps, offset):
    total = pre * taps[0:1]
    for by in range(1, taps.shape[0]):
        moved = jnp.where(offset >= by, pltpu.roll(pre, by, 0), 0.0)
        total = total + moved * taps[by : by + 1]
    return total


def to_row(column, eye):
    return jnp.sum(jnp.where(eye, column, 0.0), axis=0, keepdims=True)


def lane_of(block, lane):
    lanes = lax.broadcasted_iota(jnp.int32, block.shape, 1)
    return jnp.sum(jnp.where(lanes == lane, block, 0.0), axis=1, keepdims=True)


def softplus(value):
    return jnp.maximum(value, 0.0) + jnp.log1p(jnp.exp(-jnp.abs(value)))


def head_parts(pre_ref, taps_ref, small, head, local, heads_local, head_size, heads_all, decay_log, decay_bias, geo):
    col, row, offset, within, strict, eye = geo
    width = heads_local * head_size
    at = lambda part: slice(part * width + local * head_size, part * width + (local + 1) * head_size)
    pres = [pre_ref[:, at(part)] for part in range(3)]
    taps = [taps_ref[:, at(part)] for part in range(3)]
    sums = [conv_sum(p, t, offset) for p, t in zip(pres, taps)]
    sigs = [jax.nn.sigmoid(s) for s in sums]
    convs = [s * g for s, g in zip(sums, sigs)]
    scale_q = lax.rsqrt(jnp.sum(convs[0] * convs[0], axis=1, keepdims=True) + EPS)
    scale_k = lax.rsqrt(jnp.sum(convs[1] * convs[1], axis=1, keepdims=True) + EPS)
    query = (convs[0] * scale_q * head_size**-0.5).astype(BF)
    key = (convs[1] * scale_k).astype(BF)
    value = convs[2].astype(BF)
    shifted = lane_of(small, head) + decay_bias
    beta = jax.nn.sigmoid(lane_of(small, heads_all + head))
    rate = -jnp.exp(jnp.full_like(shifted, decay_log))
    decay = rate * softplus(shifted)
    reach = jnp.where(within, to_row(decay, eye), 0.0)
    total_col = jnp.sum(reach, axis=1, keepdims=True)
    total_row = to_row(total_col, eye)
    fall = jnp.where(within, jnp.exp(jnp.where(within, total_col - total_row, 0.0)), 0.0)
    fall_strict = jnp.where(strict, fall, 0.0)
    keys = lax.dot_general(key, key, NT, preferred_element_type=F32)
    scores = lax.dot_general(query, key, NT, preferred_element_type=F32)
    return dict(pres=pres, taps=taps, sums=sums, sigs=sigs, convs=convs, scale_q=scale_q, scale_k=scale_k,
                query=query, key=key, value=value, shifted=shifted, beta=beta, rate=rate, decay=decay,
                fall=fall, fall_strict=fall_strict, keys=keys, scores=scores,
                gate=pre_ref[:, at(3)])


def unit_inverse(lower, col, row, dot):
    size = lower.shape[0]
    both = col ^ row
    eye = (both == 0).astype(F32)
    inverse = eye - jnp.where((both == 1) & (col > row), lower, 0.0)
    reach = 2
    while reach < size:
        if reach >= 64:
            rows = []
            for first in range(0, size, 2 * reach):
                a, b, c = first, first + reach, first + 2 * reach
                low = dot(inverse[b:c, b:c], dot(lower[b:c, a:b], inverse[a:b, a:b]))
                pad_l = [jnp.zeros((2 * reach, first), F32)] if first else []
                pad_r = [jnp.zeros((2 * reach, size - c), F32)] if size > c else []
                mid = jnp.concatenate([inverse[a:b, a:b], jnp.zeros((reach, reach), F32)], axis=1)
                end = jnp.concatenate([-low, inverse[b:c, b:c]], axis=1)
                rows.append(jnp.concatenate(pad_l + [jnp.concatenate([mid, end], axis=0)] + pad_r, axis=1))
            inverse = rows[0] if len(rows) == 1 else jnp.concatenate(rows, axis=0)
        else:
            corner = jnp.where((both >= reach) & (both < 2 * reach) & (col > row), lower, 0.0)
            inverse = inverse - dot(inverse, dot(corner, inverse))
        reach *= 2
    return inverse


def forward_kernel(cfg, rank_ref, len_ref, log_ref, bias_ref, pre_ref, taps_ref, gain_ref, gated_ref, inv_ref):
    heads_local, head_size, heads_all, dot_inv, dot_use = cfg
    rows = pre_ref.shape[0]
    step = pl.program_id(0)
    col, row, offset, within, strict = layout(lambda at: len_ref[step, at], len_ref.shape[1], rows)
    eye = col == row
    geo = (col, row, offset, within, strict, eye)
    small = pre_ref[:, 4 * heads_local * head_size :]
    for local in range(heads_local):
        head = rank_ref[0] * heads_local + local
        p = head_parts(pre_ref, taps_ref, small, head, local, heads_local, head_size, heads_all, log_ref[head], bias_ref[head], geo)
        inverse = unit_inverse(p["beta"] * p["fall_strict"] * p["keys"], col, row, dot_inv)
        inv_ref[0, local] = inverse.astype(inv_ref.dtype)
        update = dot_use(inverse, p["beta"] * p["value"].astype(F32))
        mixed = dot_use(p["scores"] * p["fall"], update)
        scale = lax.rsqrt(jnp.mean(mixed * mixed, axis=1, keepdims=True) + EPS)
        gate = p["gate"]
        out = mixed * scale * gain_ref[...] * (gate * jax.nn.sigmoid(gate))
        gated_ref[:, local * head_size : (local + 1) * head_size] = out.astype(BF)


def backward_kernel(cfg, rank_ref, len_ref, log_ref, bias_ref, pre_ref, taps_ref, gain_ref, inv_ref, grad_ref,
                    dpre_ref, dtaps_ref, dgain_ref, ddecay_ref):
    heads_local, head_size, heads_all, dot_inv, dot_use = cfg
    rows = pre_ref.shape[0]
    step = pl.program_id(0)

    @pl.when(step == 0)
    def _():
        dtaps_ref[...] = jnp.zeros_like(dtaps_ref)
        dgain_ref[...] = jnp.zeros_like(dgain_ref)
        ddecay_ref[...] = jnp.zeros_like(ddecay_ref)

    col, row, offset, within, strict = layout(lambda at: len_ref[step, at], len_ref.shape[1], rows)
    eye = col == row
    geo = (col, row, offset, within, strict, eye)
    width = heads_local * head_size
    small = pre_ref[:, 4 * width :]
    dsmall = jnp.zeros_like(small)
    lanes = lax.broadcasted_iota(jnp.int32, small.shape, 1)
    row_lanes = lax.broadcasted_iota(jnp.int32, (1, ddecay_ref.shape[1]), 1)
    for local in range(heads_local):
        head = rank_ref[0] * heads_local + local
        p = head_parts(pre_ref, taps_ref, small, head, local, heads_local, head_size, heads_all, log_ref[head], bias_ref[head], geo)
        at = lambda part: slice(part * width + local * head_size, part * width + (local + 1) * head_size)
        query, key, value, beta = p["query"], p["key"], p["value"], p["beta"]
        value_f = value.astype(F32)
        inverse = halves(inv_ref[0, local].astype(F32)) if inv_ref.dtype == F32 else (inv_ref[0, local], None)
        use = (lambda a, b, d=NN: dot_use(a, b, d)) if inv_ref.dtype == F32 else (lambda a, b, d=NN: one_pass(a[0], b, d))
        update = use(inverse, beta * value_f)
        attn = p["scores"] * p["fall"]
        mixed = dot_use(attn, update)
        grad, gate, gain = grad_ref[:, local * head_size : (local + 1) * head_size].astype(F32), p["gate"], gain_ref[...]
        sig = jax.nn.sigmoid(gate)
        opened = gate * sig
        scale = lax.rsqrt(jnp.mean(mixed * mixed, axis=1, keepdims=True) + EPS)
        normed = mixed * scale
        dgate = grad * normed * gain * (sig * (1.0 + gate * (1.0 - sig)))
        dgain_ref[...] += jnp.sum(grad * opened * normed, axis=0, keepdims=True)
        dnormed = grad * opened * gain
        dmixed = scale * (dnormed - normed * jnp.mean(dnormed * normed, axis=1, keepdims=True))
        dupdate = dot_use(attn, dmixed, TN)
        dattn = jnp.where(within, dot_use(dmixed, update, NT), 0.0)
        dright = use(inverse, dupdate, TN)
        dlower = jnp.where(strict, -dot_use(dright, update, NT), 0.0)
        dvalue = beta * dright
        spread_keys = p["fall_strict"] * p["keys"]
        dbeta = jnp.sum(dright * value_f, axis=1, keepdims=True) + jnp.sum(dlower * spread_keys, axis=1, keepdims=True)
        dscores = dattn * p["fall"]
        dkeys = dlower * beta * p["fall_strict"]
        dquery = dot_use(dscores, key.astype(F32))
        dkey = dot_use(dscores, query.astype(F32), TN) + dot_use(dkeys, key.astype(F32)) + dot_use(dkeys, key.astype(F32), TN)
        pairs = dattn * attn + dlower * beta * spread_keys
        dtotal_row = to_row(jnp.sum(pairs, axis=1, keepdims=True), eye) - jnp.sum(pairs, axis=0, keepdims=True)
        later = (col <= row) & (col - offset == row_start(row, len_ref, step))
        ddecay = jnp.sum(jnp.where(later, dtotal_row, 0.0), axis=1, keepdims=True)
        dshifted = ddecay * p["rate"] * jax.nn.sigmoid(p["shifted"])
        dlog = jnp.sum(ddecay * p["decay"], axis=0, keepdims=True)
        dbias = jnp.sum(dshifted, axis=0, keepdims=True)
        ddecay_ref[0:1] += jnp.where(row_lanes == head, dlog, 0.0)
        ddecay_ref[1:2] += jnp.where(row_lanes == head, dbias, 0.0)
        dsmall = dsmall + jnp.where(lanes == head, dshifted, 0.0)
        dsmall = dsmall + jnp.where(lanes == heads_all + head, dbeta * beta * (1.0 - beta), 0.0)
        rounded = [g.astype(BF).astype(F32) for g in (dquery, dkey, dvalue)]
        cq, ck = p["convs"][0], p["convs"][1]
        gq = rounded[0] * head_size**-0.5
        dconvs = [
            p["scale_q"] * (gq - cq * (p["scale_q"] * p["scale_q"] * jnp.sum(gq * cq, axis=1, keepdims=True))),
            p["scale_k"] * (rounded[1] - ck * (p["scale_k"] * p["scale_k"] * jnp.sum(rounded[1] * ck, axis=1, keepdims=True))),
            rounded[2],
        ]
        for part in range(3):
            sig_c, total, taps, pre = p["sigs"][part], p["sums"][part], p["taps"][part], p["pres"][part]
            dsum = dconvs[part] * (sig_c * (1.0 + total * (1.0 - sig_c)))
            dpre = dsum * taps[0:1]
            dtaps_ref[0:1, at(part)] += jnp.sum(dsum * pre, axis=0, keepdims=True)
            for by in range(1, taps.shape[0]):
                kept = jnp.where(offset >= by, dsum, 0.0)
                dtaps_ref[by : by + 1, at(part)] += jnp.sum(kept * pltpu.roll(pre, by, 0), axis=0, keepdims=True)
                dpre = dpre + pltpu.roll(kept, rows - by, 0) * taps[by : by + 1]
            dpre_ref[:, at(part)] = dpre.astype(BF)
        dpre_ref[:, at(3)] = dgate.astype(BF)
    dpre_ref[:, 4 * width :] = dsmall.astype(BF)


def row_start(row, len_ref, step):
    bound = jnp.int32(0)
    start = jnp.zeros_like(row)
    for at in range(len_ref.shape[1]):
        bound = bound + len_ref[step, at]
        start = jnp.where(row >= bound, bound, start)
    return start


def mixer_forward(rank, lengths, decay_log, decay_bias, pre, taps, gain, heads_local, dot_inv=three_pass, dot_use=three_pass, inv_dtype=F32):
    buffers = lengths.shape[0]
    rows = pre.shape[0] // buffers
    head_size = gain.shape[1]
    cfg = (heads_local, head_size, decay_log.shape[0], dot_inv, dot_use)
    smem = pl.BlockSpec(memory_space=pltpu.SMEM)
    whole = lambda a: pl.BlockSpec(a.shape, lambda i: (0,) * a.ndim)
    return pl.pallas_call(
        partial(forward_kernel, cfg),
        grid=(buffers,),
        in_specs=[smem, smem, smem, smem, pl.BlockSpec((rows, pre.shape[1]), lambda i: (i, 0)), whole(taps), whole(gain)],
        out_specs=[pl.BlockSpec((rows, heads_local * head_size), lambda i: (i, 0)),
                   pl.BlockSpec((1, heads_local, rows, rows), lambda i: (i, 0, 0, 0))],
        out_shape=[jax.ShapeDtypeStruct((buffers * rows, heads_local * head_size), BF),
                   jax.ShapeDtypeStruct((buffers, heads_local, rows, rows), inv_dtype)],
        compiler_params=pltpu.CompilerParams(vmem_limit_bytes=48 << 20),
        name="mixer_forward",
    )(rank, lengths, decay_log, decay_bias, pre, taps, gain)


def mixer_backward(rank, lengths, decay_log, decay_bias, pre, taps, gain, inverse, grad, heads_local, dot_inv=three_pass, dot_use=three_pass):
    buffers = lengths.shape[0]
    rows = pre.shape[0] // buffers
    head_size = gain.shape[1]
    cfg = (heads_local, head_size, decay_log.shape[0], dot_inv, dot_use)
    smem = pl.BlockSpec(memory_space=pltpu.SMEM)
    whole = lambda s: pl.BlockSpec(s, lambda i: (0,) * len(s))
    by_rows = lambda a: pl.BlockSpec((rows, a.shape[1]), lambda i: (i, 0))
    return pl.pallas_call(
        partial(backward_kernel, cfg),
        grid=(buffers,),
        in_specs=[smem, smem, smem, smem, by_rows(pre), whole(taps.shape), whole(gain.shape),
                  pl.BlockSpec((1, heads_local, rows, rows), lambda i: (i, 0, 0, 0)), by_rows(grad)],
        out_specs=[by_rows(pre), whole(taps.shape), whole(gain.shape), whole((8, 128))],
        out_shape=[jax.ShapeDtypeStruct(pre.shape, BF), jax.ShapeDtypeStruct(taps.shape, F32),
                   jax.ShapeDtypeStruct(gain.shape, F32), jax.ShapeDtypeStruct((8, 128), F32)],
        compiler_params=pltpu.CompilerParams(vmem_limit_bytes=48 << 20),
        name="mixer_backward",
    )(rank, lengths, decay_log, decay_bias, pre, taps, gain, inverse, grad)


def dot(left, right, dims=NN):
    return lax.dot_general(left, right, dims, preferred_element_type=F32)


def place_rows(pieces, row_starts, col_starts, shape):
    whole = jnp.zeros(shape, pieces[0].dtype)
    for piece, row, col in zip(pieces, row_starts, col_starts):
        whole = lax.dynamic_update_slice(whole, piece, (row, col))
    return whole


def program(shards, ranks):
    ring = shards // 2
    reach = (ring - 1) // 2
    even = ring % 2 == 0

    def shift(value, by):
        return lax.ppermute(value, "fsdp", [(f, ((f // 2 + by) % ring) * 2 + f % 2) for f in range(shards)])

    def pair(value):
        return lax.ppermute(value, "fsdp", [(f, f ^ 1) for f in range(shards)])

    def across(value, bits):
        return lax.ppermute(value, "replica", [(r, r ^ bits) for r in range(ranks)])

    def gather_pair_first(piece):
        up = down = (piece, pair(piece))
        got = {(0, 0): up[0], (0, 1): up[1]}
        for d in range(1, reach + 1):
            up = tuple(shift(v, 1) for v in up)
            down = tuple(shift(v, -1) for v in down)
            for dy in range(2):
                got[-d % ring, dy] = up[dy]
                got[d % ring, dy] = down[dy]
        if even:
            got[ring // 2, 0] = shift(up[0], 1)
            got[ring // 2, 1] = shift(down[1], -1)
        return got

    def gather_ring_first(first, second):
        up = down = (first, second)
        got = [{}, {}]
        for at in range(2):
            got[at][0, 0] = up[at]
        for d in range(1, reach + 1):
            up = tuple(shift(v, 1) for v in up)
            down = tuple(shift(v, -1) for v in down)
            for at in range(2):
                got[at][-d % ring, 0] = up[at]
                got[at][d % ring, 0] = down[at]
        if even:
            got[0][ring // 2, 0] = shift(up[0], 1)
            got[1][ring // 2, 0] = shift(down[1], -1)
        for at in range(2):
            for (dz, _), value in list(got[at].items()):
                got[at][dz, 1] = pair(value)
        return got

    def plus(*terms):
        total = terms[0].astype(F32)
        for term in terms[1:]:
            total = total + term.astype(F32)
        return total.astype(BF)

    def ring_sum(part, by, top):
        total = part(by * top)
        for d in range(top, 0, -1):
            moved = shift(total, by)
            if d == 1:
                return moved
            total = plus(part(by * (d - 1)), moved)

    def ring_total(part, long_up):
        tops = (ring // 2 if even and long_up else reach, ring // 2 if even and not long_up else reach)
        terms = [part(0)]
        for by, top in zip((1, -1), tops):
            if top:
                terms.append(ring_sum(part, by, top))
        return plus(*terms)

    def scatter_ring_first(part):
        kept = ring_total(lambda dz: part(dz, 0), True)
        given = ring_total(lambda dz: part(dz, 1), False)
        return plus(kept, pair(given))

    def scatter_pair_first(part, long_up):
        summed = {dz % ring: plus(part(dz, 0), pair(part(dz, 1))) for dz in range(ring)}
        return ring_total(lambda dz: summed[dz % ring], long_up)

    def swap_slots(value, bits):
        shaped = value.reshape((2, 2) + value.shape[1:])
        shaped = lax.rev(shaped, [1 - at for at in range(2) if bits >> at & 1])
        return shaped.reshape(value.shape)

    def gather_rows(value):
        two = across(value, 2)
        return [value, across(value, 1), two, across(two, 1)]

    def gather_columns(value, buffers):
        rows, cols = value.shape[0] // buffers, value.shape[1]
        pieces = gather_rows(value)
        starts, offsets, parts = [], [], []
        for j, piece in enumerate(pieces):
            for k in range(buffers):
                starts.append(k * rows)
                offsets.append(j * cols)
                parts.append(lax.slice_in_dim(piece, (k ^ j) * rows, ((k ^ j) + 1) * rows, axis=0))
        blocks = [jnp.concatenate(parts[j * buffers : (j + 1) * buffers], axis=0) for j in range(ranks)]
        return jnp.concatenate(blocks, axis=1)

    def scatter_columns(blocks):
        far = plus(blocks[2], swap_slots(across(blocks[3], 1), 1))
        far = across(far, 2)
        near = across(blocks[1], 1)
        return blocks[0].astype(F32) + swap_slots(near, 1).astype(F32) + swap_slots(far, 2).astype(F32)

    def scatter_slots(slots):
        far = across(plus(slots[2], across(slots[3], 1)), 2)
        return slots[0].astype(F32) + across(slots[1], 1).astype(F32) + far.astype(F32)

    def group_sum(value):
        value = value + swap_slots(across(value, 1), 1)
        return value + swap_slots(across(value, 2), 2)

    def by_rank(pieces, rank):
        low, high = rank % 2 == 1, rank // 2 == 1
        a, b, c, d = pieces
        a, b, c, d = (jnp.where(low, *p) for p in ((b, a), (a, b), (d, c), (c, d)))
        return [jnp.where(high, *p) for p in ((c, a), (d, b), (a, c), (b, d))]

    def to_tokens(value, rank):
        pieces = [value[0]] + [across(value[j], j) for j in range(1, ranks)]
        return jnp.concatenate(by_rank(pieces, rank), axis=1)

    def on_device(
        tokens, seq_lengths, attn_gain, w_query, w_key, w_value, w_outgate, w_alpha, w_beta, conv_weight,
        decay_log, decay_bias, head_gain, w_output, mlp_gain, w_gate, w_up, w_down, cotangent,
    ):
        rows, model = tokens.shape
        heads = decay_log.shape[0]
        heads_local = heads // ranks
        width = model // ranks
        piece_rows = w_query.shape[0]
        hidden_piece = w_down.shape[0] // ranks
        taps_count = conv_weight.shape[0]
        rank = lax.axis_index("replica")
        place = lax.axis_index("fsdp")
        z, y = place // 2, place % 2

        def owner(dz, dy):
            return ((z + dz) % ring) * 2 + (y ^ dy)

        own = lambda w: lax.dynamic_slice_in_dim(w, rank * width, width, axis=1)

        conv_cols = conv_weight.size // piece_rows
        small = jnp.concatenate(
            [w_alpha, w_beta, attn_gain[:, None], mlp_gain[:, None], conv_weight.reshape(piece_rows, conv_cols)], axis=1
        )
        small = jnp.pad(small, ((0, 0), (0, 128 - small.shape[1])))
        shard_qk = jnp.concatenate([own(w_query), own(w_key)], axis=1)
        shard_v = own(w_value)
        shard_g = jnp.concatenate([own(w_outgate), small], axis=1)
        shard_o = own(w_output)
        hidden = lambda w: lax.dynamic_index_in_dim(
            w.reshape(piece_rows, shards, ranks, hidden_piece), rank, 2, keepdims=False
        ).reshape(piece_rows, shards * hidden_piece)
        shard_gu = jnp.concatenate([hidden(w_gate), hidden(w_up)], axis=1)
        shard_d = lax.dynamic_slice_in_dim(w_down, rank * hidden_piece, hidden_piece, axis=0)

        lengths_own = seq_lengths[0]
        live = (jnp.arange(rows, dtype=jnp.int32) < jnp.sum(lengths_own)).astype(F32)[:, None]
        upstream_own = cotangent * live.astype(BF)

        token_slots = gather_rows(tokens)
        lengths = jnp.concatenate(gather_rows(seq_lengths), axis=0)
        got_qk = gather_pair_first(shard_qk)
        got_v, got_g = gather_ring_first(shard_v, shard_g)
        half = width // 2
        got_o = gather_ring_first(shard_o[:, :half], shard_o[:, half:])
        upstream_slots = gather_rows(upstream_own)
        got_d = gather_ring_first(shard_d[:, : model // 2], shard_d[:, model // 2 :])
        got_gu = gather_pair_first(shard_gu)

        def placed(parts, start_of, shape):
            pieces, starts, cols = [], [], []
            for col, got in parts:
                for (dz, dy), piece in got.items():
                    pieces.append(piece)
                    starts.append(start_of(owner(dz, dy)))
                    cols.append(col)
            return place_rows(pieces, starts, cols, shape)

        whole_rows = lambda f: f * piece_rows
        per_group = shards // ranks
        group_rows = lambda f: ((f // per_group) ^ rank) * width + (f % per_group) * piece_rows
        hidden_rows = lambda f: f * hidden_piece

        in_cols = 4 * width + 128
        full_in = placed([(0, got_qk), (2 * width, got_v), (3 * width, got_g)], whole_rows, (model, in_cols))

        smalls = full_in[:, 4 * width :]
        at = 2 * heads
        gain_one = smalls[:, at].astype(F32)
        gain_two = lax.dynamic_slice_in_dim(smalls[:, at + 1], rank * width, width).astype(F32)
        conv_all = smalls[:, at + 2 : at + 2 + conv_cols].reshape(shards, taps_count, -1)
        conv_all = jnp.swapaxes(conv_all, 0, 1).reshape(taps_count, 3, model)
        taps = lax.dynamic_slice_in_dim(conv_all, rank * width, width, axis=2).reshape(taps_count, 3 * width).astype(F32)

        buffers = ranks
        group = buffers * rows
        x_all = jnp.concatenate(token_slots, axis=0)
        x_f = x_all.astype(F32)
        normed = (x_f * lax.rsqrt(jnp.mean(x_f * x_f, axis=-1, keepdims=True) + EPS) * gain_one).astype(BF)
        pre = dot(normed, full_in)
        rank_arr = rank[None].astype(jnp.int32)
        gated, inverse = mixer_forward(
            rank_arr, lengths, decay_log, decay_bias, pre, taps, head_gain[None], heads_local
        )

        gated_all = gather_columns(gated, buffers)
        full_out = placed([(0, got_o[0]), (half, got_o[1])], group_rows, (model, width))
        branch = dot(gated_all, full_out)
        resid = own(x_all).astype(F32) + branch
        branch_own = to_tokens(branch.astype(BF).reshape(buffers, rows, width), rank).astype(F32)

        scaled = (resid * gain_two).astype(BF)
        scaled_all = gather_columns(scaled, buffers)
        squares = group_sum(jnp.sum(resid * resid, axis=1).reshape(buffers, rows)).reshape(group, 1)
        inv_two = lax.rsqrt(squares / model + EPS)

        hidden_cols = shards * hidden_piece
        full_gu = placed([(0, got_gu)], group_rows, (model, 2 * hidden_cols))
        full_down = placed([(0, got_d[0]), (model // 2, got_d[1])], hidden_rows, (hidden_cols, model))
        raw = dot(scaled_all, full_gu)
        raw_gate, raw_up = raw[:, :hidden_cols], raw[:, hidden_cols:]
        gate_rows, up_rows = raw_gate * inv_two, raw_up * inv_two
        sig = jax.nn.sigmoid(gate_rows)
        opened = gate_rows * sig
        hidden_b = (opened * up_rows).astype(BF)
        upstream = jnp.concatenate(upstream_slots, axis=0)
        grad_hidden = dot(upstream, full_down, NT)
        grad_gate = (inv_two * (grad_hidden * up_rows * (sig * (1.0 + gate_rows * (1.0 - sig))))).astype(BF)
        grad_up = (inv_two * (grad_hidden * opened)).astype(BF)
        grad_gu = jnp.concatenate([grad_gate, grad_up], axis=1)
        stat = jnp.sum(raw_gate * grad_gate.astype(F32) + raw_up * grad_up.astype(F32), axis=1)
        stat = group_sum(stat.reshape(buffers, rows)).reshape(group, 1)

        blocks = [
            dot(grad_gu, full_gu[j * width : (j + 1) * width], NT).astype(BF).reshape(buffers, rows, width)
            for j in range(ranks)
        ]
        grad_two = scatter_columns(blocks).reshape(group, width)
        grad_resid = own(upstream).astype(F32) + gain_two * grad_two - resid * (inv_two * inv_two * stat / model)
        grad_mlp_gain = jnp.sum(grad_two * resid, axis=0)
        grad_branch = grad_resid.astype(BF)

        pieces_of = lambda whole, start_of, count, first, cols: (
            lambda dz, dy: lax.dynamic_slice(whole, (start_of(owner(dz, dy)), first), (count, cols))
        )
        d_gu = dot(scaled_all, grad_gu, TN).astype(BF)
        d_down = dot(hidden_b, upstream, TN).astype(BF)
        share_gu = scatter_ring_first(pieces_of(d_gu, group_rows, piece_rows, 0, 2 * hidden_cols))
        share_d = jnp.concatenate(
            [
                scatter_pair_first(pieces_of(d_down, hidden_rows, hidden_piece, side * (model // 2), model // 2), side == 0)
                for side in range(2)
            ],
            axis=1,
        )

        down = dot(hidden_b, full_down).astype(BF).reshape(buffers, rows, model)
        output = ((tokens.astype(F32) + branch_own + scatter_slots(down)) * live).astype(BF)

        blocks = [
            dot(grad_branch, full_out[j * width : (j + 1) * width], NT).astype(BF).reshape(buffers, rows, width)
            for j in range(ranks)
        ]
        grad_gated = scatter_columns(blocks).reshape(group, width)
        grad_resid_own = to_tokens(grad_branch.reshape(buffers, rows, width), rank).astype(F32)
        d_out = dot(gated_all, grad_branch, TN).astype(BF)
        d_pre, d_taps, d_head_gain, d_decay = mixer_backward(
            rank_arr, lengths, decay_log, decay_bias, pre, taps, head_gain[None], inverse, grad_gated, heads_local
        )
        d_in = dot(normed, d_pre, TN).astype(BF)
        grad_normed = dot(d_pre, full_in, NT).astype(BF).reshape(buffers, rows, model)
        share_o = jnp.concatenate(
            [scatter_pair_first(pieces_of(d_out, group_rows, piece_rows, side * half, half), side == 0) for side in range(2)],
            axis=1,
        )
        share_qk = scatter_ring_first(pieces_of(d_in, whole_rows, piece_rows, 0, 2 * width))
        share_v = scatter_pair_first(pieces_of(d_in, whole_rows, piece_rows, 2 * width, width), True)
        share_g = scatter_pair_first(pieces_of(d_in, whole_rows, piece_rows, 3 * width, width + 128), False)

        grad_one = scatter_slots(grad_normed)
        x_own = tokens.astype(F32)
        inv_one = lax.rsqrt(jnp.mean(x_own * x_own, axis=-1, keepdims=True) + EPS)
        grad_attn_gain = jnp.sum(grad_one * x_own * inv_one, axis=0)
        pulled = gain_one * grad_one
        grad_x = inv_one * pulled - x_own * (inv_one**3 * jnp.mean(pulled * x_own, axis=-1, keepdims=True))
        grad_tokens = (grad_resid_own + grad_x).astype(BF)

        own_cols = lambda value: lax.dynamic_update_slice_in_dim(
            jnp.zeros(value.shape[:-1] + (model,), F32), value, rank * width, axis=value.ndim - 1
        )
        packed = jnp.concatenate(
            [
                own_cols(d_taps.reshape(taps_count, 3, width)).reshape(-1),
                own_cols(grad_mlp_gain),
                grad_attn_gain,
                d_head_gain[0],
                d_decay[0, :heads],
                d_decay[1, :heads],
            ]
        )
        total = jnp.pad(packed, (0, -packed.size % 1024)).reshape(-1, 128)
        for bits in (1, 2):
            total = total + across(total, bits)
        bits = 1
        while bits < shards:
            total = total + lax.ppermute(total, "fsdp", [(f, f ^ bits) for f in range(shards)])
            bits *= 2
        total = total.reshape(-1)
        conv_size = taps_count * 3 * model
        sum_conv = total[:conv_size].reshape(taps_count, shards, -1)
        sum_conv = lax.dynamic_index_in_dim(sum_conv, place, 1, keepdims=False)
        at = conv_size
        sum_mlp_gain = lax.dynamic_slice_in_dim(total, at + place * piece_rows, piece_rows)
        sum_attn_gain = lax.dynamic_slice_in_dim(total, at + model + place * piece_rows, piece_rows)
        at += 2 * model
        sum_head_gain = total[at : at + head_gain.size]
        at += head_gain.size
        sum_log, sum_bias = total[at : at + heads], total[at + heads : at + 2 * heads]

        wide = lambda share: jnp.concatenate(by_rank(gather_rows(share), rank), axis=1).astype(F32)
        qk_all = by_rank(gather_rows(share_qk), rank)
        out_query = jnp.concatenate([p[:, :width] for p in qk_all], axis=1).astype(F32)
        out_key = jnp.concatenate([p[:, width:] for p in qk_all], axis=1).astype(F32)
        g_all = gather_rows(share_g)
        out_outgate = jnp.concatenate([p[:, :width] for p in by_rank(g_all, rank)], axis=1).astype(F32)
        low = (g_all[0][:, width:].astype(F32) + g_all[1][:, width:]) + (g_all[2][:, width:].astype(F32) + g_all[3][:, width:])
        out_alpha, out_beta = low[:, :heads], low[:, heads : 2 * heads]
        gu_all = by_rank(gather_rows(share_gu), rank)
        unhide = lambda first: (
            jnp.stack([p[:, first : first + hidden_cols].reshape(piece_rows, shards, hidden_piece) for p in gu_all], axis=2)
            .reshape(piece_rows, shards * ranks * hidden_piece)
            .astype(F32)
        )
        out_down = jnp.concatenate(by_rank(gather_rows(share_d), rank), axis=0).astype(F32)
        return (
            output, grad_tokens, sum_attn_gain, out_query, out_key, wide(share_v), out_outgate, out_alpha, out_beta,
            sum_conv, sum_log, sum_bias, sum_head_gain, wide(share_o), sum_mlp_gain, unhide(0), unhide(hidden_cols), out_down,
        )

    return on_device


def solution(mesh):
    rows, cols = P("fsdp", None), P("fsdp")
    tokens = P(("replica", "fsdp"), None)
    return jax.shard_map(
        program(mesh.shape["fsdp"], mesh.shape["replica"]),
        mesh=mesh,
        in_specs=(
            tokens, tokens, cols, rows, rows, rows, rows, rows, rows, P(None, "fsdp"), P(), P(), P(), rows, cols,
            rows, rows, rows, tokens,
        ),
        out_specs=(
            tokens, tokens, cols, rows, rows, rows, rows, rows, rows, P(None, "fsdp"), P(), P(), P(), rows, cols,
            rows, rows, rows,
        ),
        check_vma=False,
    )
```

```python
import copy
from functools import partial

import jax
import jax.numpy as jnp
import numpy as np
from jax import lax
from jax.experimental import pallas as pl
from jax.experimental.pallas import tpu as pltpu
from jax.sharding import PartitionSpec as P

EPS = 1e-06
BF = jnp.bfloat16
F32 = jnp.float32
NN = (((1,), (0,)), ((), ()))
NT = (((1,), (1,)), ((), ()))
TN = (((0,), (0,)), ((), ()))


def one_pass(left, right, dims=NN):
    return lax.dot_general(left.astype(BF), right.astype(BF), dims, preferred_element_type=F32)


def halves(value):
    high = value.astype(BF)
    return high, (value - high.astype(F32)).astype(BF)


def three_pass(left, right, dims=NN):
    lh, ll = left if isinstance(left, tuple) else halves(left)
    rh, rl = right if isinstance(right, tuple) else halves(right)
    total = lax.dot_general(lh, rh, dims, preferred_element_type=F32)
    total = total + lax.dot_general(lh, rl, dims, preferred_element_type=F32)
    return total + lax.dot_general(ll, rh, dims, preferred_element_type=F32)


def layout(length_of, count, rows):
    col = lax.broadcasted_iota(jnp.int32, (rows, 1), 0)
    row = lax.broadcasted_iota(jnp.int32, (1, rows), 1)
    bound = jnp.int32(0)
    start_col = jnp.zeros_like(col)
    start_row = jnp.zeros_like(row)
    for at in range(count):
        bound = bound + length_of(at)
        start_col = jnp.where(col >= bound, bound, start_col)
        start_row = jnp.where(row >= bound, bound, start_row)
    same = start_col == start_row
    within = same & (col >= row)
    strict = same & (col > row)
    return col, row, col - start_col, within, strict


def conv_sum(pre, taps, offset):
    total = pre * taps[0:1]
    for by in range(1, taps.shape[0]):
        moved = jnp.where(offset >= by, pltpu.roll(pre, by, 0), 0.0)
        total = total + moved * taps[by : by + 1]
    return total


def to_row(column, eye):
    return jnp.sum(jnp.where(eye, column, 0.0), axis=0, keepdims=True)


def lane_of(block, lane):
    lanes = lax.broadcasted_iota(jnp.int32, block.shape, 1)
    return jnp.sum(jnp.where(lanes == lane, block, 0.0), axis=1, keepdims=True)


def softplus(value):
    return jnp.maximum(value, 0.0) + jnp.log1p(jnp.exp(-jnp.abs(value)))


def head_parts(pre_ref, taps_ref, small, head, local, heads_local, head_size, heads_all, decay_log, decay_bias, geo):
    col, row, offset, within, strict, eye = geo
    width = heads_local * head_size
    at = lambda part: slice(part * width + local * head_size, part * width + (local + 1) * head_size)
    pres = [pre_ref[:, at(part)] for part in range(3)]
    taps = [taps_ref[:, at(part)] for part in range(3)]
    sums = [conv_sum(p, t, offset) for p, t in zip(pres, taps)]
    sigs = [jax.nn.sigmoid(s) for s in sums]
    convs = [s * g for s, g in zip(sums, sigs)]
    scale_q = lax.rsqrt(jnp.sum(convs[0] * convs[0], axis=1, keepdims=True) + EPS)
    scale_k = lax.rsqrt(jnp.sum(convs[1] * convs[1], axis=1, keepdims=True) + EPS)
    query = (convs[0] * scale_q * head_size**-0.5).astype(BF)
    key = (convs[1] * scale_k).astype(BF)
    value = convs[2].astype(BF)
    shifted = lane_of(small, head) + decay_bias
    beta = jax.nn.sigmoid(lane_of(small, heads_all + head))
    rate = -jnp.exp(jnp.full_like(shifted, decay_log))
    decay = rate * softplus(shifted)
    reach = jnp.where(within, to_row(decay, eye), 0.0)
    total_col = jnp.sum(reach, axis=1, keepdims=True)
    total_row = to_row(total_col, eye)
    fall = jnp.where(within, jnp.exp(jnp.where(within, total_col - total_row, 0.0)), 0.0)
    fall_strict = jnp.where(strict, fall, 0.0)
    keys = lax.dot_general(key, key, NT, preferred_element_type=F32)
    scores = lax.dot_general(query, key, NT, preferred_element_type=F32)
    return dict(pres=pres, taps=taps, sums=sums, sigs=sigs, convs=convs, scale_q=scale_q, scale_k=scale_k,
                query=query, key=key, value=value, shifted=shifted, beta=beta, rate=rate, decay=decay,
                fall=fall, fall_strict=fall_strict, keys=keys, scores=scores,
                gate=pre_ref[:, at(3)])


def two_pass(left, right, dims=NN):
    high, low = halves(left)
    return lax.dot_general(high, right, dims, preferred_element_type=F32) + lax.dot_general(
        low, right, dims, preferred_element_type=F32
    )


def unit_inverses(lowers):
    half = lowers[0].shape[0] // 2
    col = lax.broadcasted_iota(jnp.int32, (half, half), 0)
    row = lax.broadcasted_iota(jnp.int32, (half, half), 1)
    both = jnp.where(col > row, col ^ row, 0)
    eye = (col == row).astype(F32)
    blocks = [low[at : at + half, at : at + half] for low in lowers for at in (0, half)]
    inverses = [eye - jnp.where(both == 1, block, 0.0) for block in blocks]
    reach = 2
    while reach < half:
        corner = (both >= reach) & (both < 2 * reach)
        small = [inverse.astype(BF) for inverse in inverses]
        steps = [one_pass(jnp.where(corner, block, 0.0), inverse) for block, inverse in zip(blocks, small)]
        inverses = [inverse - one_pass(s, step) for inverse, s, step in zip(inverses, small, steps)]
        reach *= 2
    small = [inverse.astype(BF) for inverse in inverses]
    steps = [one_pass(low[half:, :half], small[2 * at]) for at, low in enumerate(lowers)]
    corners = [one_pass(small[2 * at + 1], step) for at, step in enumerate(steps)]
    zero = jnp.zeros((half, half), BF)
    return [
        jnp.concatenate(
            [
                jnp.concatenate([small[2 * at], zero], axis=1),
                jnp.concatenate([(-corner).astype(BF), small[2 * at + 1]], axis=1),
            ],
            axis=0,
        )
        for at, corner in enumerate(corners)
    ]


def solve(lower, inverse, right, dims=NN):
    result = one_pass(inverse, right, dims)
    return result + one_pass(inverse, right - result - three_pass(lower, result, dims), dims)


def forward_kernel(cfg, step, rank_ref, len_ref, log_ref, bias_ref, pre_ref, taps_ref, gain_ref, *refs):
    heads_local, head_size, heads_all, dot_use = cfg
    rows = pre_ref.shape[0]
    gated_ref, inv_ref = refs[-2:]
    col, row, offset, within, strict = layout(lambda at: len_ref[step, at], len_ref.shape[1], rows)
    eye = col == row
    geo = (col, row, offset, within, strict, eye)
    small = pre_ref[:, 4 * heads_local * head_size :]
    parts = []
    for local in range(heads_local):
        head = rank_ref[0] * heads_local + local
        parts.append(head_parts(pre_ref, taps_ref, small, head, local, heads_local, head_size, heads_all, log_ref[head], bias_ref[head], geo))
    lowers = [p["beta"] * p["fall_strict"] * p["keys"] for p in parts]
    inverses = unit_inverses(lowers)
    for local, (p, lower, inverse) in enumerate(zip(parts, lowers, inverses)):
        inv_ref[0, local] = inverse
        update = solve(lower, inverse, p["beta"] * p["value"].astype(F32))
        mixed = dot_use(p["scores"] * p["fall"], update)
        scale = lax.rsqrt(jnp.mean(mixed * mixed, axis=1, keepdims=True) + EPS)
        gate = p["gate"]
        out = mixed * scale * gain_ref[...] * (gate * jax.nn.sigmoid(gate))
        gated_ref[:, local * head_size : (local + 1) * head_size] = out.astype(BF)


def backward_kernel(cfg, step, rank_ref, len_ref, log_ref, bias_ref, pre_ref, taps_ref, gain_ref, inv_ref, own_ref, near_ref, far_ref, *refs):
    heads_local, head_size, heads_all, dot_use = cfg
    rows = pre_ref.shape[0]
    dpre_ref, dtaps_ref, dgain_ref, ddecay_ref = refs[-4:]
    for sum_ref, at in zip((dtaps_ref, dgain_ref, ddecay_ref), range(1, 4)):
        sum_ref[...] = refs[at][...] if step else jnp.zeros_like(sum_ref)

    col, row, offset, within, strict = layout(lambda at: len_ref[step, at], len_ref.shape[1], rows)
    eye = col == row
    geo = (col, row, offset, within, strict, eye)
    width = heads_local * head_size
    small = pre_ref[:, 4 * width :]
    dsmall = jnp.zeros_like(small)
    lanes = lax.broadcasted_iota(jnp.int32, small.shape, 1)
    row_lanes = lax.broadcasted_iota(jnp.int32, (1, ddecay_ref.shape[1]), 1)
    for local in range(heads_local):
        head = rank_ref[0] * heads_local + local
        p = head_parts(pre_ref, taps_ref, small, head, local, heads_local, head_size, heads_all, log_ref[head], bias_ref[head], geo)
        at = lambda part: slice(part * width + local * head_size, part * width + (local + 1) * head_size)
        query, key, value, beta = p["query"], p["key"], p["value"], p["beta"]
        value_f = value.astype(F32)
        inverse = inv_ref[0, local]
        spread_keys = p["fall_strict"] * p["keys"]
        lower = beta * spread_keys
        update = solve(lower, inverse, beta * value_f)
        attn = p["scores"] * p["fall"]
        mixed = dot_use(attn, update)
        lanes_of = slice(local * head_size, (local + 1) * head_size)
        grad = own_ref[:, lanes_of].astype(F32) + near_ref[:, lanes_of].astype(F32) + far_ref[:, lanes_of].astype(F32)
        gate, gain = p["gate"], gain_ref[...]
        sig = jax.nn.sigmoid(gate)
        opened = gate * sig
        scale = lax.rsqrt(jnp.mean(mixed * mixed, axis=1, keepdims=True) + EPS)
        normed = mixed * scale
        dgate = grad * normed * gain * (sig * (1.0 + gate * (1.0 - sig)))
        dgain_ref[...] += jnp.sum(grad * opened * normed, axis=0, keepdims=True)
        dnormed = grad * opened * gain
        dmixed = scale * (dnormed - normed * jnp.mean(dnormed * normed, axis=1, keepdims=True))
        dupdate = dot_use(attn, dmixed, TN)
        dattn = jnp.where(within, dot_use(dmixed, update, NT), 0.0)
        dright = solve(lower, inverse, dupdate, TN)
        dlower = jnp.where(strict, -dot_use(dright, update, NT), 0.0)
        dvalue = beta * dright
        dbeta = jnp.sum(dright * value_f, axis=1, keepdims=True) + jnp.sum(dlower * spread_keys, axis=1, keepdims=True)
        dscores = dattn * p["fall"]
        dkeys = dlower * beta * p["fall_strict"]
        dquery = two_pass(dscores, key)
        dkey = two_pass(dscores, query, TN) + two_pass(dkeys, key) + two_pass(dkeys, key, TN)
        pairs = dattn * attn + dlower * lower
        dtotal_row = to_row(jnp.sum(pairs, axis=1, keepdims=True), eye) - jnp.sum(pairs, axis=0, keepdims=True)
        later = (col <= row) & (col - offset == row_start(row, len_ref, step))
        ddecay = jnp.sum(jnp.where(later, dtotal_row, 0.0), axis=1, keepdims=True)
        dshifted = ddecay * p["rate"] * jax.nn.sigmoid(p["shifted"])
        dlog = jnp.sum(ddecay * p["decay"], axis=0, keepdims=True)
        dbias = jnp.sum(dshifted, axis=0, keepdims=True)
        ddecay_ref[0:1] += jnp.where(row_lanes == head, dlog, 0.0)
        ddecay_ref[1:2] += jnp.where(row_lanes == head, dbias, 0.0)
        dsmall = dsmall + jnp.where(lanes == head, dshifted, 0.0)
        dsmall = dsmall + jnp.where(lanes == heads_all + head, dbeta * beta * (1.0 - beta), 0.0)
        rounded = [g.astype(BF).astype(F32) for g in (dquery, dkey, dvalue)]
        cq, ck = p["convs"][0], p["convs"][1]
        gq = rounded[0] * head_size**-0.5
        dconvs = [
            p["scale_q"] * (gq - cq * (p["scale_q"] * p["scale_q"] * jnp.sum(gq * cq, axis=1, keepdims=True))),
            p["scale_k"] * (rounded[1] - ck * (p["scale_k"] * p["scale_k"] * jnp.sum(rounded[1] * ck, axis=1, keepdims=True))),
            rounded[2],
        ]
        for part in range(3):
            sig_c, total, taps, pre = p["sigs"][part], p["sums"][part], p["taps"][part], p["pres"][part]
            dsum = dconvs[part] * (sig_c * (1.0 + total * (1.0 - sig_c)))
            dpre = dsum * taps[0:1]
            dtaps_ref[0:1, at(part)] += jnp.sum(dsum * pre, axis=0, keepdims=True)
            for by in range(1, taps.shape[0]):
                kept = jnp.where(offset >= by, dsum, 0.0)
                dtaps_ref[by : by + 1, at(part)] += jnp.sum(kept * pltpu.roll(pre, by, 0), axis=0, keepdims=True)
                dpre = dpre + pltpu.roll(kept, rows - by, 0) * taps[by : by + 1]
            dpre_ref[:, at(part)] = dpre.astype(BF)
        dpre_ref[:, at(3)] = dgate.astype(BF)
    dpre_ref[:, 4 * width :] = dsmall.astype(BF)


def row_start(row, len_ref, step):
    bound = jnp.int32(0)
    start = jnp.zeros_like(row)
    for at in range(len_ref.shape[1]):
        bound = bound + len_ref[step, at]
        start = jnp.where(row >= bound, bound, start)
    return start


def mixer_forward(at, rank, lengths, decay_log, decay_bias, pre, taps, gain, heads_local, made):
    buffers = lengths.shape[0]
    rows = pre.shape[0] // buffers
    head_size = gain.shape[1]
    cfg = (heads_local, head_size, decay_log.shape[0], three_pass)
    smem = pl.BlockSpec(memory_space=pltpu.SMEM)
    entire = lambda a: pl.BlockSpec(a.shape, lambda i, rank: (0,) * a.ndim)
    by_rows = lambda cols: pl.BlockSpec((rows, cols), lambda i, rank: (at ^ rank[0], 0))
    width = heads_local * head_size
    return pl.pallas_call(
        partial(forward_kernel, cfg, at),
        grid_spec=pltpu.PrefetchScalarGridSpec(
            num_scalar_prefetch=1,
            grid=(1,),
            in_specs=[smem, smem, smem, by_rows(pre.shape[1]), entire(taps), entire(gain)]
            + [pl.BlockSpec(memory_space=pl.ANY)] * len(made),
            out_specs=[by_rows(width), pl.BlockSpec((1, heads_local, rows, rows), lambda i, rank: (at ^ rank[0], 0, 0, 0))],
        ),
        out_shape=[jax.ShapeDtypeStruct((buffers * rows, width), BF),
                   jax.ShapeDtypeStruct((buffers, heads_local, rows, rows), BF)],
        input_output_aliases={7 + n: n for n in range(len(made))},
        compiler_params=pltpu.CompilerParams(vmem_limit_bytes=48 << 20),
        cost_estimate=pl.CostEstimate(flops=int(19e6), bytes_accessed=1 << 10, transcendentals=0),
        name="mixer_forward",
    )(rank, lengths, decay_log, decay_bias, pre, taps, gain, *made)


def mixer_backward(at, rank, lengths, decay_log, decay_bias, pre, taps, gain, inverse, grads, heads_local, made):
    buffers = lengths.shape[0]
    rows = pre.shape[0] // buffers
    head_size = gain.shape[1]
    cfg = (heads_local, head_size, decay_log.shape[0], three_pass)
    smem = pl.BlockSpec(memory_space=pltpu.SMEM)
    entire = lambda s: pl.BlockSpec(s, lambda i, rank: (0,) * len(s))
    by_rows = lambda a: pl.BlockSpec((rows, a.shape[1]), lambda i, rank: (at ^ rank[0], 0))
    sums = [entire(taps.shape), entire(gain.shape), entire((8, 128))]
    return pl.pallas_call(
        partial(backward_kernel, cfg, at),
        grid_spec=pltpu.PrefetchScalarGridSpec(
            num_scalar_prefetch=1,
            grid=(1,),
            in_specs=[smem, smem, smem, by_rows(pre), entire(taps.shape), entire(gain.shape),
                      pl.BlockSpec((1, heads_local, rows, rows), lambda i, rank: (at ^ rank[0], 0, 0, 0)),
                      *[by_rows(g) for g in grads]]
            + ([pl.BlockSpec(memory_space=pl.ANY)] + sums if made else []),
            out_specs=[by_rows(pre)] + sums,
        ),
        out_shape=[jax.ShapeDtypeStruct(pre.shape, BF), jax.ShapeDtypeStruct(taps.shape, F32),
                   jax.ShapeDtypeStruct(gain.shape, F32), jax.ShapeDtypeStruct((8, 128), F32)],
        input_output_aliases={11: 0} if made else {},
        compiler_params=pltpu.CompilerParams(vmem_limit_bytes=48 << 20),
        cost_estimate=pl.CostEstimate(flops=int(12e6), bytes_accessed=1 << 10, transcendentals=0),
        name="mixer_backward",
    )(rank, lengths, decay_log, decay_bias, pre, taps, gain, inverse, *grads, *made)


def dot(left, right, dims=NN):
    return lax.dot_general(left, right, dims, preferred_element_type=F32)


ANY = pl.BlockSpec(memory_space=pl.ANY)
LIMIT = 56 << 20
INV, OWN, RANK = 0, 1, 2


def whole(array):
    return pl.BlockSpec(array.shape, lambda i, info: (0,) * array.ndim)


def to_col(row, eye):
    return jnp.sum(jnp.where(eye, row, 0.0), axis=1, keepdims=True)


def diagonal(rows):
    return lax.broadcasted_iota(jnp.int32, (rows, rows), 0) == lax.broadcasted_iota(jnp.int32, (rows, rows), 1)


class Pieces:
    def __init__(self, parts, rows, first=0, columns=None):
        self.arrays, self.starts = [a for a, _ in parts], [jnp.asarray(s, jnp.int32) for _, s in parts]
        self.first, self.shape = first, (rows, columns or parts[0][0].shape[1])

    def copies(self, info, base, sources, target, sem, sem_base):
        made = []
        for at, source in enumerate(sources):
            rows, cols = source.shape[0], self.shape[1]
            source = source.at[:, pl.ds(self.first, cols)]
            place = target.at[pl.ds(pl.multiple_of(info[base + at], 16), rows)]
            made.append(pltpu.make_async_copy(source, place, sem.at[sem_base + at]))
        return made


def kernel_call(body, name, cost, grid, info, ins, weights, outs, scratch=(), onto=()):
    lead = len(info)
    scalars = jnp.stack([jnp.asarray(v, jnp.int32) for v in info] + [s for w in weights for s in w.starts])
    counts = [len(w.arrays) for w in weights]
    total = sum(counts)

    def kernel(info_ref, *refs):
        in_refs, refs = refs[: len(ins)], refs[len(ins) :]
        piece_refs, refs = refs[:total], refs[total:]
        refs = refs[len(onto) :]
        out_refs, refs = refs[: len(outs)], refs[len(outs) :]
        full_refs, refs = refs[: len(weights)], refs[len(weights) :]
        extra = refs[: len(scratch)]
        if total:
            sem = refs[len(scratch)]

            @pl.when(pl.program_id(0) == 0)
            def _():
                made, at = [], 0
                for w, full, count in zip(weights, full_refs, counts):
                    made += w.copies(info_ref, lead + at, piece_refs[at : at + count], full, sem, at)
                    at += count
                for move in made:
                    move.start()
                for move in made:
                    move.wait()

        body(info_ref, in_refs, full_refs, out_refs, extra)

    return pl.pallas_call(
        kernel,
        grid_spec=pltpu.PrefetchScalarGridSpec(
            num_scalar_prefetch=1,
            grid=grid,
            in_specs=[spec for _, spec in ins] + [ANY] * (total + len(onto)),
            out_specs=[spec for _, _, spec in outs],
            scratch_shapes=[pltpu.VMEM(w.shape, BF) for w in weights]
            + list(scratch)
            + ([pltpu.SemaphoreType.DMA((total,))] if total else []),
        ),
        out_shape=[jax.ShapeDtypeStruct(shape, kind) for shape, kind, _ in outs],
        input_output_aliases={1 + len(ins) + total + at: at for at in range(len(onto))},
        compiler_params=pltpu.CompilerParams(vmem_limit_bytes=LIMIT),
        cost_estimate=estimate(cost),
        name=name,
    )(scalars, *[a for a, _ in ins], *[p for w in weights for p in w.arrays], *onto)


COST = 1e6


def estimate(micros):
    return pl.CostEstimate(flops=int(micros * COST), bytes_accessed=1 << 10, transcendentals=0)


def program(shards, ranks):
    ring = shards // 2
    by_line = ring == 4

    def after(value, *others):
        return lax.optimization_barrier((value,) + others)[0] if others else value

    last = {}

    def send(lane, value, axis, pairs):
        sent = lax.ppermute(after(value, *last.get(lane, ())), axis, pairs)
        last[lane] = (sent,)
        return sent

    def pair(value):
        return send("pair", value, "fsdp", [(f, f ^ 1) for f in range(shards)])

    def across(value, bits):
        return send(("rank", min(bits, 2)), value, "replica", [(r, r ^ bits) for r in range(ranks)])

    def hop(value, by, sources):
        return send(by, value, "fsdp", [(2 * at + y, 2 * (at + by) + y) for at in sources for y in range(2)])

    def gather(piece, z, y, *ahead):
        got = [(piece, z * 2 + y)]

        def exchange(value, at):
            other = pair(value)
            got.extend([(value, at * 2 + y), (other, at * 2 + (y ^ 1))] if at is not z else [(other, at * 2 + (y ^ 1))])
            return other

        up1, down1 = hop(piece, 1, (0, 1, 2)), hop(piece, -1, (1, 2, 3))
        other = exchange(piece, z)
        up2, down2 = hop(after(up1, other, *ahead), 1, (1, 2)), hop(after(down1, other, *ahead), -1, (1, 2))
        other = exchange(jnp.where(z == 3, up1, down1), jnp.where(z == 3, 2, z + 1))
        up3, down3 = hop(after(up2, other), 1, (2,)), hop(after(down2, other), -1, (1,))
        exchange(jnp.where(z >= 2, up2, down2), (z + 2) % 4)
        far = jnp.where(z == 0, down3, jnp.where(z == 3, up3, up1))
        exchange(far, jnp.where(z == 0, 3, jnp.where(z == 3, 0, z - 1)))
        return got

    def gather_whole(piece):
        return lax.all_gather(piece, "fsdp", axis=0, tiled=True)

    def plus(*terms):
        total = terms[0].astype(F32)
        for term in terms[1:]:
            total = total + term.astype(F32)
        return total.astype(BF)

    def line_sum(part):
        up = down = None
        for k in range(1, 4):
            up = hop(plus(part(4 - k), *([] if up is None else [up])), 1, range(k))
            down = hop(plus(part(k), *([] if down is None else [down])), -1, range(4 - k, 4))
        return [up, down]

    def scatter_whole(value):
        return lax.psum_scatter(value, "fsdp", scatter_dimension=0, tiled=True)

    def scatter(part):
        given = pair(jnp.stack([part(dz, 1) for dz in range(4)]))
        return lambda *events: finish([plus(after(part(dz, 0), *events), given[dz]) for dz in range(4)])

    def finish(summed):
        return plus(summed[0], *line_sum(lambda dz: summed[dz]))

    def scatter_along(value):
        lines = [[2 * at + y for at in range(ring)] for y in range(2)]
        flat = value.reshape((-1,) + value.shape[2:])
        return lax.psum_scatter(flat, "fsdp", scatter_dimension=0, tiled=True, axis_index_groups=lines)

    def gather_group(value):
        two = across(value, 2)
        return [value, across(value, 1), two, across(two, 1)]

    def scatter_group(parts):
        far = across(plus(parts[2], across(parts[3], 1)), 2)
        return parts[0], across(parts[1], 1), far

    def by_rank(pieces, rank):
        low, high = rank % 2 == 1, rank // 2 == 1
        a, b, c, d = pieces
        a, b, c, d = (jnp.where(low, *p) for p in ((b, a), (a, b), (d, c), (c, d)))
        return [jnp.where(high, *p) for p in ((c, a), (d, b), (a, c), (b, d))]

    def on_device(
        tokens, seq_lengths, attn_gain, w_query, w_key, w_value, w_outgate, w_alpha, w_beta, conv_weight,
        decay_log, decay_bias, head_gain, w_output, mlp_gain, w_gate, w_up, w_down, cotangent,
    ):
        rows, model = tokens.shape
        heads = decay_log.shape[0]
        heads_local = heads // ranks
        width = model // ranks
        piece_rows = w_query.shape[0]
        hidden_piece = w_down.shape[0] // ranks
        hidden_cols = shards * hidden_piece
        taps_count = conv_weight.shape[0]
        buffers = ranks
        group = buffers * rows
        rank = lax.axis_index("replica")
        place = lax.axis_index("fsdp")
        z, y = place // 2, place % 2

        def owner(dz, dy):
            return ((z + dz) % ring) * 2 + (y ^ dy)

        own = lambda w: lax.dynamic_slice_in_dim(w, rank * width, width, axis=1)

        conv_parts = conv_weight.shape[1] // piece_rows
        conv_cols = conv_weight.T.reshape(conv_parts, piece_rows, taps_count)
        conv_cols = jnp.swapaxes(conv_cols, 0, 1).reshape(piece_rows, conv_parts * taps_count)
        small = jnp.concatenate([w_alpha, w_beta, attn_gain[:, None], mlp_gain[:, None], conv_cols], axis=1)
        small = jnp.pad(small, ((0, 0), (0, 128 - small.shape[1])))
        shard_in = jnp.concatenate([own(w_query), own(w_key), own(w_value), own(w_outgate), small, own(w_output)], axis=1)
        hidden = lambda w: lax.dynamic_index_in_dim(
            w.reshape(piece_rows, shards, ranks, hidden_piece), rank, 2, keepdims=False
        ).reshape(piece_rows, hidden_cols)
        shard_gu = jnp.concatenate([hidden(w_gate), hidden(w_up)], axis=1)
        shard_d = lax.dynamic_slice_in_dim(w_down, rank * hidden_piece, hidden_piece, axis=0)

        live = (jnp.arange(rows, dtype=jnp.int32) < jnp.sum(seq_lengths[0])).astype(F32)[:, None]
        note = jnp.pad(seq_lengths.astype(BF), ((0, 15), (0, model - seq_lengths.shape[1])))
        tokens_noted = jnp.concatenate([tokens, note], axis=0)
        upstream_own = cotangent * live.astype(BF)

        token_slots = gather_group(tokens_noted)
        whole_in = gather_whole(shard_in)
        upstream_slots = gather_group(upstream_own)
        lengths = jnp.stack([t[rows, : seq_lengths.shape[1]] for t in token_slots]).astype(jnp.int32)
        if by_line:
            got_d = [(piece, f * hidden_piece) for piece, f in gather(shard_d, z, y, token_slots[2])]
        else:
            got_d = [(gather_whole(shard_d), 0)]
        ahead = [*token_slots[1:], *upstream_slots[1:], *[piece for piece, _ in got_d[1:]]]
        whole_gu = gather_whole(after(shard_gu, whole_in, *ahead))

        in_cols = 4 * width + 128
        full_in = Pieces([(whole_in, 0)], model, 0, in_cols)
        full_out = Pieces([(whole_in, 0)], model, in_cols, width)
        full_gu = Pieces([(whole_gu, 0)], model)
        full_down = Pieces(got_d, hidden_cols)

        info = [rank]
        by_slot = lambda cols: pl.BlockSpec((rows, cols), lambda i, info: (i ^ info[0], 0))
        by_row = lambda cols: pl.BlockSpec((rows, cols), lambda i, info: (i, 0))
        a_row = pl.BlockSpec((1, 1, rows), lambda i, info: (i, 0, 0))
        lanes_of = lambda info, j: pl.ds(pl.multiple_of((info[0] ^ j) * width, 128), width)
        own_lanes = lambda info: lanes_of(info, 0)
        gain_rows = 16

        def enter_body(info, ins, weights, outs, extra):
            (w_ref,) = weights
            x_refs = ins
            pre_ref, normed_ref, x_own_ref, lane_ref = outs
            (x_ref,) = extra
            step = pl.program_id(0)

            @pl.when(step == 0)
            def _():
                picked = lax.broadcasted_iota(jnp.int32, (gain_rows, 128), 0) + 2 * heads
                picked = (picked == lax.broadcasted_iota(jnp.int32, (gain_rows, 128), 1)).astype(BF)
                for first in range(0, model, 256):
                    block = w_ref[first : first + 256, 4 * width :]
                    lane_ref[:, first : first + 256] = dot(picked, block, NT)

            for j in range(len(x_refs)):
                @pl.when(step == j)
                def _():
                    x_ref[...] = x_refs[j][:rows]

            x_own_ref[...] = x_ref[:, own_lanes(info)]
            x = x_ref[...].astype(F32)
            scale = lax.rsqrt(jnp.mean(x * x, axis=1, keepdims=True) + EPS)
            normed = (x * scale * lane_ref[0:1]).astype(BF)
            normed_ref[...] = normed
            pre_ref[...] = dot(normed, w_ref[...])

        slot = pl.BlockSpec((rows, model), lambda i, info: (0, 0))
        entered = []
        for first in (0, 2):
            some = lambda cols: pl.BlockSpec((rows, cols), lambda i, info: ((i + info[1]) ^ info[0], 0))
            entered.append(kernel_call(
                enter_body, "enter", 11, (2,), [rank, first],
                [(x, whole(x)) for x in token_slots[first : first + 2]], [full_in],
                [
                    ((group, in_cols), F32, some(in_cols)), ((group, model), BF, some(model)),
                    ((group, width), BF, some(width)),
                    ((gain_rows, model), F32, pl.BlockSpec((gain_rows, model), lambda i, info: (0, 0))),
                ],
                [pltpu.VMEM((rows, model), BF)], entered[0][:3] if entered else (),
            ))
        pre, normed, x_cols = entered[1][:3]
        lanes = entered[0][3]
        gain_one = lanes[0]
        own_gain = pl.BlockSpec((1, width), lambda i, info: (0, 0))
        gain_two = lax.dynamic_slice_in_dim(lanes[1:2], rank * width, width, axis=1)
        conv_all = lanes[2 : 2 + conv_parts * taps_count].reshape(conv_parts, taps_count, shards, piece_rows)
        conv_all = conv_all.transpose(1, 2, 0, 3).reshape(taps_count, 3, model)
        taps = lax.dynamic_slice_in_dim(conv_all, rank * width, width, axis=2).reshape(taps_count, 3 * width)

        rank_arr = rank[None].astype(jnp.int32)
        made = ()
        for at in range(buffers):
            source = entered[at // 2][0]
            if at == 2:
                source = pre
            made = mixer_forward(
                at, rank_arr, lengths, decay_log, decay_bias, source, taps, head_gain[None], heads_local, made
            )
        gated, inverse = made

        def leave_body(info, ins, weights, outs, extra):
            (w_ref,) = weights
            x_ref, gain_ref = ins[ranks:]
            all_ref, resid_ref, branch_ref, scaled_ref, square_ref = outs
            for j in range(ranks):
                all_ref[:, lanes_of(info, j)] = ins[j][...]
            branch = dot(all_ref[...], w_ref[...])
            resid = x_ref[...].astype(F32) + branch
            resid_ref[...] = resid
            branch_ref[...] = branch
            scaled_ref[...] = (resid * gain_ref[...]).astype(BF)
            square_ref[0] = to_row(jnp.sum(resid * resid, axis=1, keepdims=True), diagonal(rows))

        gated_all, resid, branch, scaled, square = kernel_call(
            leave_body, "leave", 9, (buffers,), info,
            [(g, by_row(width)) for g in gather_group(gated)] + [(x_cols, by_row(width)), (gain_two, own_gain)],
            [full_out],
            [
                ((group, model), BF, by_row(model)), ((group, width), F32, by_row(width)),
                ((group, width), F32, by_row(width)), ((group, width), BF, by_row(width)),
                ((buffers, 1, rows), F32, a_row),
            ],
        )
        squares = gather_group(square)

        def inverse_scale(square_refs):
            total = square_refs[0][0]
            for ref in square_refs[1:]:
                total = total + ref[0]
            return lax.rsqrt(to_col(total, diagonal(rows)) / model + EPS)

        def hidden_body(info, ins, weights, outs, extra):
            w_ref, d_ref = weights
            all_ref, hidden_ref, grad_ref, stat_ref, u_ref, u_own_ref = outs
            for j in range(ranks):
                @pl.when(pl.program_id(0) ^ info[0] == j)
                def _():
                    u_ref[...] = ins[2 * ranks + j][...]

            u_own_ref[...] = u_ref[:, own_lanes(info)]
            for j in range(ranks):
                all_ref[:, lanes_of(info, j)] = ins[j][...]
            inv = inverse_scale(ins[ranks : 2 * ranks])
            raw_gate = dot(all_ref[...], w_ref[:, :hidden_cols])
            raw_up = dot(all_ref[...], w_ref[:, hidden_cols:])
            grad_hidden = dot(u_ref[...], d_ref[...], NT)
            gate, up = raw_gate * inv, raw_up * inv
            sig = jax.nn.sigmoid(gate)
            opened = gate * sig
            hidden_ref[...] = (opened * up).astype(BF)
            grad_hidden = grad_hidden * inv
            grad_gate = (grad_hidden * up * (sig * (1.0 + gate * (1.0 - sig)))).astype(BF)
            grad_up = (grad_hidden * opened).astype(BF)
            grad_ref[:, :hidden_cols] = grad_gate
            grad_ref[:, hidden_cols:] = grad_up
            stat = jnp.sum(raw_gate * grad_gate.astype(F32) + raw_up * grad_up.astype(F32), axis=1, keepdims=True)
            stat_ref[0] = to_row(stat, diagonal(rows))

        scaled_all, hidden_b, grad_gu, stat, upstream, u_cols = kernel_call(
            hidden_body, "hidden", 33, (buffers,), info,
            [(s, by_row(width)) for s in gather_group(scaled)] + [(s, a_row) for s in squares]
            + [(u, slot) for u in upstream_slots],
            [full_gu, full_down],
            [
                ((group, model), BF, by_row(model)), ((group, hidden_cols), BF, by_row(hidden_cols)),
                ((group, 2 * hidden_cols), BF, by_row(2 * hidden_cols)), ((buffers, 1, rows), F32, a_row),
                ((group, model), BF, by_row(model)), ((group, width), BF, by_row(width)),
            ],
        )
        stats = gather_group(stat)

        def back_body(info, ins, weights, outs, extra):
            for j in range(ranks):
                outs[j][...] = dot(ins[0][...], weights[0][lanes_of(info, j)], NT).astype(BF)

        d_gu = dot(scaled_all, grad_gu, TN).astype(BF)
        share_gu = scatter_whole(d_gu)
        parts = kernel_call(
            back_body, "back", 19, (buffers,), info, [(after(grad_gu, d_gu), by_row(2 * hidden_cols))], [full_gu],
            [((group, width), BF, by_row(width))] * ranks,
        )
        terms_two = scatter_group(parts)

        def scattered(value, piece):
            if not by_line:
                return lambda *events: scatter_whole(value)
            return scatter(lambda dz, dy: lax.dynamic_slice_in_dim(value, owner(dz, dy) * piece, piece, axis=0))

        d_down = dot(hidden_b, upstream, TN).astype(BF)
        end_d = scattered(d_down, hidden_piece)

        def turn_body(info, ins, weights, outs, extra):
            (w_ref,) = weights
            own_ref, near_ref, far_ref, resid_ref, u_ref, gain_ref = ins[:6]
            grad_ref, out_refs, gain_out_ref = outs[0], outs[1 : 1 + ranks], outs[1 + ranks]

            @pl.when(pl.program_id(0) == 0)
            def _():
                gain_out_ref[...] = jnp.zeros_like(gain_out_ref)

            grad_two = own_ref[...].astype(F32) + near_ref[...].astype(F32) + far_ref[...].astype(F32)
            resid = resid_ref[...]
            inv = inverse_scale(ins[6 : 6 + ranks])
            total = ins[6 + ranks][0]
            for ref in ins[7 + ranks :]:
                total = total + ref[0]
            stat = to_col(total, diagonal(rows))
            gain_out_ref[...] += jnp.sum(grad_two * resid, axis=0, keepdims=True)
            grad = u_ref[...].astype(F32) + gain_ref[...] * grad_two - resid * (inv * inv * stat / model)
            grad = grad.astype(BF)
            grad_ref[...] = grad
            for j in range(ranks):
                out_refs[j][...] = dot(grad, w_ref[lanes_of(info, j)], NT).astype(BF)

        turned = kernel_call(
            turn_body, "turn", 9, (buffers,), info,
            [(t, by_row(width)) for t in terms_two]
            + [(after(resid, d_down), by_row(width)), (u_cols, by_row(width)), (gain_two, own_gain)]
            + [(s, a_row) for s in squares] + [(s, a_row) for s in stats],
            [full_out],
            [((group, width), BF, by_row(width))] * (1 + ranks) + [((1, width), F32, own_gain)],
        )
        grad_branch, grad_mlp_gain = turned[0], turned[1 + ranks][0]
        terms_gated = scatter_group(turned[1 : 1 + ranks])
        d_out = dot(gated_all, grad_branch, TN).astype(BF)
        own_block = lambda value, j: lax.dynamic_slice_in_dim(value, (rank ^ j) * rows, rows, axis=0)

        def to_tokens(value):
            pieces = [own_block(value, 0)] + [across(own_block(value, j), j) for j in range(1, ranks)]
            return jnp.concatenate(by_rank(pieces, rank), axis=1).astype(F32)

        def down_body(info, ins, weights, outs, extra):
            (full,) = extra
            full[...] = dot(ins[0][...], weights[0][...])
            full[:, own_lanes(info)] += ins[1][...]
            for j in range(ranks):
                @pl.when(pl.program_id(0) == j)
                def _():
                    outs[j][...] = full[...].astype(BF)

        down = kernel_call(
            down_body, "down", 14, (ranks,), info, [(hidden_b, by_slot(hidden_cols)), (branch, by_slot(width))], [full_down],
            [((rows, model), BF, slot)] * ranks, [pltpu.VMEM((rows, model), F32)],
        )
        down_terms = scatter_group(down)
        output = tokens.astype(F32)
        for term in down_terms:
            output = output + term.astype(F32)
        output = (output * live).astype(BF)
        grad_resid_own = to_tokens(grad_branch)

        made = ()
        ahead = [(d_out, *down), (), (down_terms[2],), (grad_resid_own,)]
        for at in range(buffers):
            made = mixer_backward(
                at, rank_arr, lengths, decay_log, decay_bias, after(pre, *ahead[at]), taps, head_gain[None], inverse,
                terms_gated, heads_local, made,
            )
        d_pre, d_taps, d_head_gain, d_decay = made
        cuts = ((0, 2 * width), (2 * width, 2 * width + 128))
        d_in = [dot(normed, d_pre[:, first : first + count], TN).astype(BF) for first, count in cuts]
        in_sums = []
        for value in d_in:
            if by_line:
                placed = value.reshape(ring, 2, piece_rows, value.shape[1])
                given = pair(lax.dynamic_index_in_dim(placed, 1 - y, 1, keepdims=False))
                in_sums.append(plus(lax.dynamic_index_in_dim(placed, y, 1, keepdims=False), given))
            else:
                in_sums.append(value)
        along = scatter_along if by_line else scatter_whole
        share_a = along(after(in_sums[0], share_gu))
        share_b = along(after(in_sums[1], share_a))
        end_o = scattered(d_out, piece_rows)

        def first_body(info, ins, weights, outs, extra):
            result = dot(ins[0][...], weights[0][...], NT).astype(BF)
            for j in range(ranks):
                @pl.when(pl.program_id(0) == j)
                def _():
                    outs[j][...] = result

        grad_slots = kernel_call(
            first_body, "first", 19, (ranks,), info, [(after(d_pre, *d_in), by_slot(in_cols))], [full_in],
            [((rows, model), BF, slot)] * ranks,
        )
        grad_one = sum(t.astype(F32) for t in scatter_group(grad_slots))
        gu_slots = gather_group(share_gu)
        share_d = end_d(grad_slots[0], down[0])
        share_o = end_o(grad_slots[0], down[0])
        d_slots, o_slots = gather_group(share_d), gather_group(share_o)
        x_own = tokens.astype(F32)
        inv_one = lax.rsqrt(jnp.mean(x_own * x_own, axis=-1, keepdims=True) + EPS)
        grad_attn_gain = jnp.sum(grad_one * x_own * inv_one, axis=0)
        pulled = gain_one * grad_one
        grad_x = inv_one * pulled - x_own * (inv_one**3 * jnp.mean(pulled * x_own, axis=-1, keepdims=True))
        grad_tokens = (grad_resid_own + grad_x).astype(BF)

        own_cols = lambda value: lax.dynamic_update_slice_in_dim(
            jnp.zeros(value.shape[:-1] + (model,), F32), value, rank * width, axis=value.ndim - 1
        )
        packed = jnp.concatenate(
            [
                own_cols(d_taps.reshape(taps_count, 3, width)).reshape(-1),
                own_cols(grad_mlp_gain),
                grad_attn_gain,
                d_head_gain[0],
                d_decay[0, :heads],
                d_decay[1, :heads],
            ]
        )
        total = jnp.pad(packed, (0, -packed.size % 1024)).reshape(-1, 128)
        for bits in (1, 2):
            total = total + lax.ppermute(total, "replica", [(r, r ^ bits) for r in range(ranks)])
        bits = 1
        while bits < shards:
            total = total + lax.ppermute(total, "fsdp", [(f, f ^ bits) for f in range(shards)])
            bits *= 2
        total = total.reshape(-1)
        conv_size = taps_count * 3 * model
        sum_conv = total[:conv_size].reshape(taps_count, shards, -1)
        sum_conv = lax.dynamic_index_in_dim(sum_conv, place, 1, keepdims=False)
        at = conv_size
        sum_mlp_gain = lax.dynamic_slice_in_dim(total, at + place * piece_rows, piece_rows)
        sum_attn_gain = lax.dynamic_slice_in_dim(total, at + model + place * piece_rows, piece_rows)
        at += 2 * model
        sum_head_gain = total[at : at + head_gain.size]
        at += head_gain.size
        sum_log, sum_bias = total[at : at + heads], total[at + heads : at + 2 * heads]

        gu_all = by_rank(gu_slots, rank)
        unhide = lambda first: (
            jnp.stack([p[:, first : first + hidden_cols].reshape(piece_rows, shards, hidden_piece) for p in gu_all], axis=2)
            .reshape(piece_rows, shards * ranks * hidden_piece)
            .astype(F32)
        )
        out_gate, out_up = unhide(0), unhide(hidden_cols)
        out_down = jnp.concatenate(by_rank(d_slots, rank), axis=0).astype(F32)
        out_output = jnp.concatenate(by_rank(o_slots, rank), axis=1).astype(F32)
        a_all = by_rank(gather_group(share_a), rank)
        out_query, out_key = (
            jnp.concatenate([p[:, at * width : (at + 1) * width] for p in a_all], axis=1).astype(F32) for at in range(2)
        )
        finished = (out_gate, out_up, out_down, out_output, output, grad_tokens, sum_conv, out_query, out_key)
        share_b, *finished = lax.optimization_barrier((share_b, *finished))
        out_gate, out_up, out_down, out_output, output, grad_tokens, sum_conv, out_query, out_key = finished
        b_slots = gather_group(share_b)
        b_all = by_rank(b_slots, rank)
        out_value, out_outgate = (
            jnp.concatenate([p[:, at * width : (at + 1) * width] for p in b_all], axis=1).astype(F32) for at in range(2)
        )
        low = [p[:, 2 * width :].astype(F32) for p in b_slots]
        low = (low[0] + low[1]) + (low[2] + low[3])
        out_alpha, out_beta = low[:, :heads], low[:, heads : 2 * heads]
        return (
            output, grad_tokens, sum_attn_gain, out_query, out_key, out_value, out_outgate, out_alpha, out_beta,
            sum_conv, sum_log, sum_bias, sum_head_gain, out_output, sum_mlp_gain, out_gate, out_up, out_down,
        )

    return on_device


def solution(mesh):
    rows, cols = P("fsdp", None), P("fsdp")
    tokens = P(("replica", "fsdp"), None)
    return jax.shard_map(
        program(mesh.shape["fsdp"], mesh.shape["replica"]),
        mesh=mesh,
        in_specs=(
            tokens, tokens, cols, rows, rows, rows, rows, rows, rows, P(None, "fsdp"), P(), P(), P(), rows, cols,
            rows, rows, rows, tokens,
        ),
        out_specs=(
            tokens, tokens, cols, rows, rows, rows, rows, rows, rows, P(None, "fsdp"), P(), P(), P(), rows, cols,
            rows, rows, rows,
        ),
        check_vma=False,
    )
```

```python
import copy
from functools import partial

import jax
import jax.numpy as jnp
import numpy as np
from jax import lax
from jax.experimental import pallas as pl
from jax.experimental.pallas import tpu as pltpu
from jax.sharding import PartitionSpec as P

EPS = 1e-06
BF = jnp.bfloat16
F32 = jnp.float32
NN = (((1,), (0,)), ((), ()))
NT = (((1,), (1,)), ((), ()))
TN = (((0,), (0,)), ((), ()))


def one_pass(left, right, dims=NN):
    return lax.dot_general(left.astype(BF), right.astype(BF), dims, preferred_element_type=F32)


def halves(value):
    high = value.astype(BF)
    return high, (value - high.astype(F32)).astype(BF)


def three_pass(left, right, dims=NN):
    lh, ll = left if isinstance(left, tuple) else halves(left)
    rh, rl = right if isinstance(right, tuple) else halves(right)
    total = lax.dot_general(lh, rh, dims, preferred_element_type=F32)
    total = total + lax.dot_general(lh, rl, dims, preferred_element_type=F32)
    return total + lax.dot_general(ll, rh, dims, preferred_element_type=F32)


def layout(length_of, count, rows):
    col = lax.broadcasted_iota(jnp.int32, (rows, 1), 0)
    row = lax.broadcasted_iota(jnp.int32, (1, rows), 1)
    bound = jnp.int32(0)
    start_col = jnp.zeros_like(col)
    start_row = jnp.zeros_like(row)
    for at in range(count):
        bound = bound + length_of(at)
        start_col = jnp.where(col >= bound, bound, start_col)
        start_row = jnp.where(row >= bound, bound, start_row)
    same = start_col == start_row
    within = same & (col >= row)
    strict = same & (col > row)
    return col, row, col - start_col, within, strict


def conv_sum(pre, taps, offset):
    total = pre * taps[0:1]
    for by in range(1, taps.shape[0]):
        moved = jnp.where(offset >= by, pltpu.roll(pre, by, 0), 0.0)
        total = total + moved * taps[by : by + 1]
    return total


def to_row(column, eye):
    return jnp.sum(jnp.where(eye, column, 0.0), axis=0, keepdims=True)


def lane_of(block, lane):
    lanes = lax.broadcasted_iota(jnp.int32, block.shape, 1)
    return jnp.sum(jnp.where(lanes == lane, block, 0.0), axis=1, keepdims=True)


def softplus(value):
    return jnp.maximum(value, 0.0) + jnp.log1p(jnp.exp(-jnp.abs(value)))


def head_parts(pre_ref, taps_ref, small, head, local, heads_local, head_size, heads_all, decay_log, decay_bias, geo):
    col, row, offset, within, strict, eye = geo
    width = heads_local * head_size
    at = lambda part: slice(part * width + local * head_size, part * width + (local + 1) * head_size)
    pres = [pre_ref[:, at(part)] for part in range(3)]
    taps = [taps_ref[:, at(part)] for part in range(3)]
    sums = [conv_sum(p, t, offset) for p, t in zip(pres, taps)]
    sigs = [jax.nn.sigmoid(s) for s in sums]
    convs = [s * g for s, g in zip(sums, sigs)]
    scale_q = lax.rsqrt(jnp.sum(convs[0] * convs[0], axis=1, keepdims=True) + EPS)
    scale_k = lax.rsqrt(jnp.sum(convs[1] * convs[1], axis=1, keepdims=True) + EPS)
    query = (convs[0] * scale_q * head_size**-0.5).astype(BF)
    key = (convs[1] * scale_k).astype(BF)
    value = convs[2].astype(BF)
    shifted = lane_of(small, head) + decay_bias
    beta = jax.nn.sigmoid(lane_of(small, heads_all + head))
    rate = -jnp.exp(jnp.full_like(shifted, decay_log))
    decay = rate * softplus(shifted)
    reach = jnp.where(within, to_row(decay, eye), 0.0)
    total_col = jnp.sum(reach, axis=1, keepdims=True)
    total_row = to_row(total_col, eye)
    fall = jnp.where(within, jnp.exp(jnp.where(within, total_col - total_row, 0.0)), 0.0)
    fall_strict = jnp.where(strict, fall, 0.0)
    keys = lax.dot_general(key, key, NT, preferred_element_type=F32)
    scores = lax.dot_general(query, key, NT, preferred_element_type=F32)
    return dict(pres=pres, taps=taps, sums=sums, sigs=sigs, convs=convs, scale_q=scale_q, scale_k=scale_k,
                query=query, key=key, value=value, shifted=shifted, beta=beta, rate=rate, decay=decay,
                fall=fall, fall_strict=fall_strict, keys=keys, scores=scores,
                gate=pre_ref[:, at(3)])


def two_pass(left, right, dims=NN):
    high, low = halves(left)
    return lax.dot_general(high, right, dims, preferred_element_type=F32) + lax.dot_general(
        low, right, dims, preferred_element_type=F32
    )


def unit_inverses(lowers):
    half = lowers[0].shape[0] // 2
    col = lax.broadcasted_iota(jnp.int32, (half, half), 0)
    row = lax.broadcasted_iota(jnp.int32, (half, half), 1)
    both = jnp.where(col > row, col ^ row, 0)
    eye = (col == row).astype(F32)
    blocks = [low[at : at + half, at : at + half] for low in lowers for at in (0, half)]
    inverses = [eye - jnp.where(both == 1, block, 0.0) for block in blocks]
    reach = 2
    while reach < half:
        corner = (both >= reach) & (both < 2 * reach)
        small = [inverse.astype(BF) for inverse in inverses]
        steps = [one_pass(jnp.where(corner, block, 0.0), inverse) for block, inverse in zip(blocks, small)]
        inverses = [inverse - one_pass(s, step) for inverse, s, step in zip(inverses, small, steps)]
        reach *= 2
    small = [inverse.astype(BF) for inverse in inverses]
    steps = [one_pass(low[half:, :half], small[2 * at]) for at, low in enumerate(lowers)]
    corners = [one_pass(small[2 * at + 1], step) for at, step in enumerate(steps)]
    zero = jnp.zeros((half, half), BF)
    return [
        jnp.concatenate(
            [
                jnp.concatenate([small[2 * at], zero], axis=1),
                jnp.concatenate([(-corner).astype(BF), small[2 * at + 1]], axis=1),
            ],
            axis=0,
        )
        for at, corner in enumerate(corners)
    ]


def solve_all(lowers, inverses, rights, dims=NN):
    results = [one_pass(inverse, right, dims) for inverse, right in zip(inverses, rights)]
    lefts = [
        right - result - three_pass(lower, result, dims) for lower, right, result in zip(lowers, rights, results)
    ]
    return [result + one_pass(inverse, left, dims) for result, inverse, left in zip(results, inverses, lefts)]


def forward_kernel(cfg, step, rank_ref, len_ref, log_ref, bias_ref, pre_ref, taps_ref, gain_ref, *refs):
    heads_local, head_size, heads_all, dot_use = cfg
    rows = pre_ref.shape[0]
    gated_ref, inv_ref = refs[-2:]
    col, row, offset, within, strict = layout(lambda at: len_ref[step, at], len_ref.shape[1], rows)
    eye = col == row
    geo = (col, row, offset, within, strict, eye)
    small = pre_ref[:, 4 * heads_local * head_size :]
    parts = []
    for local in range(heads_local):
        head = rank_ref[0] * heads_local + local
        parts.append(head_parts(pre_ref, taps_ref, small, head, local, heads_local, head_size, heads_all, log_ref[head], bias_ref[head], geo))
    lowers = [p["beta"] * p["fall_strict"] * p["keys"] for p in parts]
    inverses = unit_inverses(lowers)
    updates = solve_all(lowers, inverses, [p["beta"] * p["value"].astype(F32) for p in parts])
    mixeds = [dot_use(p["scores"] * p["fall"], update) for p, update in zip(parts, updates)]
    for local, (p, inverse, mixed) in enumerate(zip(parts, inverses, mixeds)):
        inv_ref[0, local] = inverse
        scale = lax.rsqrt(jnp.mean(mixed * mixed, axis=1, keepdims=True) + EPS)
        gate = p["gate"]
        out = mixed * scale * gain_ref[...] * (gate * jax.nn.sigmoid(gate))
        gated_ref[:, local * head_size : (local + 1) * head_size] = out.astype(BF)


def backward_kernel(cfg, step, rank_ref, len_ref, log_ref, bias_ref, pre_ref, taps_ref, gain_ref, inv_ref, own_ref, near_ref, far_ref, *refs):
    heads_local, head_size, heads_all, dot_use = cfg
    rows = pre_ref.shape[0]
    dpre_ref, dtaps_ref, dgain_ref, ddecay_ref = refs[-4:]
    for sum_ref, at in zip((dtaps_ref, dgain_ref, ddecay_ref), range(1, 4)):
        sum_ref[...] = refs[at][...] if step else jnp.zeros_like(sum_ref)

    col, row, offset, within, strict = layout(lambda at: len_ref[step, at], len_ref.shape[1], rows)
    eye = col == row
    geo = (col, row, offset, within, strict, eye)
    width = heads_local * head_size
    small = pre_ref[:, 4 * width :]
    dsmall = jnp.zeros_like(small)
    lanes = lax.broadcasted_iota(jnp.int32, small.shape, 1)
    row_lanes = lax.broadcasted_iota(jnp.int32, (1, ddecay_ref.shape[1]), 1)
    everyone = range(heads_local)
    heads = [rank_ref[0] * heads_local + local for local in everyone]
    at = lambda part, local: slice(part * width + local * head_size, part * width + (local + 1) * head_size)
    ps = [
        head_parts(pre_ref, taps_ref, small, head, local, heads_local, head_size, heads_all, log_ref[head], bias_ref[head], geo)
        for local, head in zip(everyone, heads)
    ]
    gain = gain_ref[...]
    betas = [p["beta"] for p in ps]
    values = [p["value"].astype(F32) for p in ps]
    inverses = [inv_ref[0, local] for local in everyone]
    spreads = [p["fall_strict"] * p["keys"] for p in ps]
    lowers = [beta * spread for beta, spread in zip(betas, spreads)]
    attns = [p["scores"] * p["fall"] for p in ps]
    updates = solve_all(lowers, inverses, [beta * value for beta, value in zip(betas, values)])
    mixeds = [dot_use(attn, update) for attn, update in zip(attns, updates)]
    dmixeds = []
    for local, (p, mixed) in enumerate(zip(ps, mixeds)):
        lanes_of = slice(local * head_size, (local + 1) * head_size)
        grad = own_ref[:, lanes_of].astype(F32) + near_ref[:, lanes_of].astype(F32) + far_ref[:, lanes_of].astype(F32)
        gate = p["gate"]
        sig = jax.nn.sigmoid(gate)
        opened = gate * sig
        scale = lax.rsqrt(jnp.mean(mixed * mixed, axis=1, keepdims=True) + EPS)
        normed = mixed * scale
        dpre_ref[:, at(3, local)] = (grad * normed * gain * (sig * (1.0 + gate * (1.0 - sig)))).astype(BF)
        dgain_ref[...] += jnp.sum(grad * opened * normed, axis=0, keepdims=True)
        dnormed = grad * opened * gain
        dmixeds.append(scale * (dnormed - normed * jnp.mean(dnormed * normed, axis=1, keepdims=True)))
    dupdates = [dot_use(attn, dmixed, TN) for attn, dmixed in zip(attns, dmixeds)]
    dattns = [jnp.where(within, dot_use(dmixed, update, NT), 0.0) for dmixed, update in zip(dmixeds, updates)]
    drights = solve_all(lowers, inverses, dupdates, TN)
    dlowers = [jnp.where(strict, -dot_use(dright, update, NT), 0.0) for dright, update in zip(drights, updates)]
    dscores = [dattn * p["fall"] for dattn, p in zip(dattns, ps)]
    dkeys = [dlower * beta * p["fall_strict"] for dlower, beta, p in zip(dlowers, betas, ps)]
    dqueries = [two_pass(dscore, p["key"]) for dscore, p in zip(dscores, ps)]
    dkey_rows = [
        two_pass(dscore, p["query"], TN) + two_pass(dkey, p["key"]) + two_pass(dkey, p["key"], TN)
        for dscore, dkey, p in zip(dscores, dkeys, ps)
    ]
    later = (col <= row) & (col - offset == row_start(row, len_ref, step))
    for local, (head, p) in enumerate(zip(heads, ps)):
        beta, dright, dlower, dattn = betas[local], drights[local], dlowers[local], dattns[local]
        dbeta = jnp.sum(dright * values[local], axis=1, keepdims=True)
        dbeta = dbeta + jnp.sum(dlower * spreads[local], axis=1, keepdims=True)
        pairs = dattn * attns[local] + dlower * lowers[local]
        dtotal_row = to_row(jnp.sum(pairs, axis=1, keepdims=True), eye) - jnp.sum(pairs, axis=0, keepdims=True)
        ddecay = jnp.sum(jnp.where(later, dtotal_row, 0.0), axis=1, keepdims=True)
        dshifted = ddecay * p["rate"] * jax.nn.sigmoid(p["shifted"])
        dlog = jnp.sum(ddecay * p["decay"], axis=0, keepdims=True)
        dbias = jnp.sum(dshifted, axis=0, keepdims=True)
        ddecay_ref[0:1] += jnp.where(row_lanes == head, dlog, 0.0)
        ddecay_ref[1:2] += jnp.where(row_lanes == head, dbias, 0.0)
        dsmall = dsmall + jnp.where(lanes == head, dshifted, 0.0)
        dsmall = dsmall + jnp.where(lanes == heads_all + head, dbeta * beta * (1.0 - beta), 0.0)
        rounded = [g.astype(BF).astype(F32) for g in (dqueries[local], dkey_rows[local], beta * dright)]
        cq, ck = p["convs"][0], p["convs"][1]
        gq = rounded[0] * head_size**-0.5
        dconvs = [
            p["scale_q"] * (gq - cq * (p["scale_q"] * p["scale_q"] * jnp.sum(gq * cq, axis=1, keepdims=True))),
            p["scale_k"] * (rounded[1] - ck * (p["scale_k"] * p["scale_k"] * jnp.sum(rounded[1] * ck, axis=1, keepdims=True))),
            rounded[2],
        ]
        for part in range(3):
            sig_c, total, taps, pre = p["sigs"][part], p["sums"][part], p["taps"][part], p["pres"][part]
            dsum = dconvs[part] * (sig_c * (1.0 + total * (1.0 - sig_c)))
            dpre = dsum * taps[0:1]
            dtaps_ref[0:1, at(part, local)] += jnp.sum(dsum * pre, axis=0, keepdims=True)
            for by in range(1, taps.shape[0]):
                kept = jnp.where(offset >= by, dsum, 0.0)
                dtaps_ref[by : by + 1, at(part, local)] += jnp.sum(kept * pltpu.roll(pre, by, 0), axis=0, keepdims=True)
                dpre = dpre + pltpu.roll(kept, rows - by, 0) * taps[by : by + 1]
            dpre_ref[:, at(part, local)] = dpre.astype(BF)
    dpre_ref[:, 4 * width :] = dsmall.astype(BF)


def row_start(row, len_ref, step):
    bound = jnp.int32(0)
    start = jnp.zeros_like(row)
    for at in range(len_ref.shape[1]):
        bound = bound + len_ref[step, at]
        start = jnp.where(row >= bound, bound, start)
    return start


def mixer_forward(at, rank, lengths, decay_log, decay_bias, pre, taps, gain, heads_local, made):
    buffers = lengths.shape[0]
    rows = pre.shape[0] // buffers
    head_size = gain.shape[1]
    cfg = (heads_local, head_size, decay_log.shape[0], three_pass)
    smem = pl.BlockSpec(memory_space=pltpu.SMEM)
    entire = lambda a: pl.BlockSpec(a.shape, lambda i, rank: (0,) * a.ndim)
    by_rows = lambda cols: pl.BlockSpec((rows, cols), lambda i, rank: (at ^ rank[0], 0))
    width = heads_local * head_size
    return pl.pallas_call(
        partial(forward_kernel, cfg, at),
        grid_spec=pltpu.PrefetchScalarGridSpec(
            num_scalar_prefetch=1,
            grid=(1,),
            in_specs=[smem, smem, smem, by_rows(pre.shape[1]), entire(taps), entire(gain)]
            + [pl.BlockSpec(memory_space=pl.ANY)] * len(made),
            out_specs=[by_rows(width), pl.BlockSpec((1, heads_local, rows, rows), lambda i, rank: (at ^ rank[0], 0, 0, 0))],
        ),
        out_shape=[jax.ShapeDtypeStruct((buffers * rows, width), BF),
                   jax.ShapeDtypeStruct((buffers, heads_local, rows, rows), BF)],
        input_output_aliases={7 + n: n for n in range(len(made))},
        compiler_params=pltpu.CompilerParams(vmem_limit_bytes=48 << 20),
        cost_estimate=pl.CostEstimate(flops=int(19e6), bytes_accessed=1 << 10, transcendentals=0),
        name="mixer_forward",
    )(rank, lengths, decay_log, decay_bias, pre, taps, gain, *made)


def mixer_backward(at, rank, lengths, decay_log, decay_bias, pre, taps, gain, inverse, grads, heads_local, made):
    buffers = lengths.shape[0]
    rows = pre.shape[0] // buffers
    head_size = gain.shape[1]
    cfg = (heads_local, head_size, decay_log.shape[0], three_pass)
    smem = pl.BlockSpec(memory_space=pltpu.SMEM)
    entire = lambda s: pl.BlockSpec(s, lambda i, rank: (0,) * len(s))
    by_rows = lambda a: pl.BlockSpec((rows, a.shape[1]), lambda i, rank: (at ^ rank[0], 0))
    sums = [entire(taps.shape), entire(gain.shape), entire((8, 128))]
    return pl.pallas_call(
        partial(backward_kernel, cfg, at),
        grid_spec=pltpu.PrefetchScalarGridSpec(
            num_scalar_prefetch=1,
            grid=(1,),
            in_specs=[smem, smem, smem, by_rows(pre), entire(taps.shape), entire(gain.shape),
                      pl.BlockSpec((1, heads_local, rows, rows), lambda i, rank: (at ^ rank[0], 0, 0, 0)),
                      *[by_rows(g) for g in grads]]
            + ([pl.BlockSpec(memory_space=pl.ANY)] + sums if made else []),
            out_specs=[by_rows(pre)] + sums,
        ),
        out_shape=[jax.ShapeDtypeStruct(pre.shape, BF), jax.ShapeDtypeStruct(taps.shape, F32),
                   jax.ShapeDtypeStruct(gain.shape, F32), jax.ShapeDtypeStruct((8, 128), F32)],
        input_output_aliases={11: 0} if made else {},
        compiler_params=pltpu.CompilerParams(vmem_limit_bytes=48 << 20),
        cost_estimate=pl.CostEstimate(flops=int(12e6), bytes_accessed=1 << 10, transcendentals=0),
        name="mixer_backward",
    )(rank, lengths, decay_log, decay_bias, pre, taps, gain, inverse, *grads, *made)


def dot(left, right, dims=NN):
    return lax.dot_general(left, right, dims, preferred_element_type=F32)


ANY = pl.BlockSpec(memory_space=pl.ANY)
LIMIT = 56 << 20
INV, OWN, RANK = 0, 1, 2


def whole(array):
    return pl.BlockSpec(array.shape, lambda i, info: (0,) * array.ndim)


def to_col(row, eye):
    return jnp.sum(jnp.where(eye, row, 0.0), axis=1, keepdims=True)


def diagonal(rows):
    return lax.broadcasted_iota(jnp.int32, (rows, rows), 0) == lax.broadcasted_iota(jnp.int32, (rows, rows), 1)


class Pieces:
    def __init__(self, parts, rows, first=0, columns=None):
        self.arrays, self.starts = [a for a, _ in parts], [jnp.asarray(s, jnp.int32) for _, s in parts]
        self.first, self.shape = first, (rows, columns or parts[0][0].shape[1])

    def copies(self, info, base, sources, target, sem, sem_base):
        made = []
        for at, source in enumerate(sources):
            rows, cols = source.shape[0], self.shape[1]
            source = source.at[:, pl.ds(self.first, cols)]
            place = target.at[pl.ds(pl.multiple_of(info[base + at], 16), rows)]
            made.append(pltpu.make_async_copy(source, place, sem.at[sem_base + at]))
        return made


def kernel_call(body, name, cost, grid, info, ins, weights, outs, scratch=(), onto=()):
    lead = len(info)
    scalars = jnp.stack([jnp.asarray(v, jnp.int32) for v in info] + [s for w in weights for s in w.starts])
    counts = [len(w.arrays) for w in weights]
    total = sum(counts)

    def kernel(info_ref, *refs):
        in_refs, refs = refs[: len(ins)], refs[len(ins) :]
        piece_refs, refs = refs[:total], refs[total:]
        refs = refs[len(onto) :]
        out_refs, refs = refs[: len(outs)], refs[len(outs) :]
        full_refs, refs = refs[: len(weights)], refs[len(weights) :]
        extra = refs[: len(scratch)]
        if total:
            sem = refs[len(scratch)]

            @pl.when(pl.program_id(0) == 0)
            def _():
                made, at = [], 0
                for w, full, count in zip(weights, full_refs, counts):
                    made += w.copies(info_ref, lead + at, piece_refs[at : at + count], full, sem, at)
                    at += count
                for move in made:
                    move.start()
                for move in made:
                    move.wait()

        body(info_ref, in_refs, full_refs, out_refs, extra)

    return pl.pallas_call(
        kernel,
        grid_spec=pltpu.PrefetchScalarGridSpec(
            num_scalar_prefetch=1,
            grid=grid,
            in_specs=[spec for _, spec in ins] + [ANY] * (total + len(onto)),
            out_specs=[spec for _, _, spec in outs],
            scratch_shapes=[pltpu.VMEM(w.shape, BF) for w in weights]
            + list(scratch)
            + ([pltpu.SemaphoreType.DMA((total,))] if total else []),
        ),
        out_shape=[jax.ShapeDtypeStruct(shape, kind) for shape, kind, _ in outs],
        input_output_aliases={1 + len(ins) + total + at: at for at in range(len(onto))},
        compiler_params=pltpu.CompilerParams(vmem_limit_bytes=LIMIT),
        cost_estimate=estimate(cost),
        name=name,
    )(scalars, *[a for a, _ in ins], *[p for w in weights for p in w.arrays], *onto)


COST = 1e6


def estimate(micros):
    return pl.CostEstimate(flops=int(micros * COST), bytes_accessed=1 << 10, transcendentals=0)


def program(shards, ranks):
    ring = shards // 2
    by_line = ring == 4

    def after(value, *others):
        return lax.optimization_barrier((value,) + others)[0] if others else value

    last, leaving = {}, {}

    def send(lane, value, axis, pairs):
        sent = lax.ppermute(after(value, *last.get(lane, ())), axis, pairs)
        last[lane] = (sent,)
        return sent

    def pair(value, lane="pair"):
        return send(lane, value, "fsdp", [(f, f ^ 1) for f in range(shards)])

    def across(value, bits):
        return send(("rank", min(bits, 2)), value, "replica", [(r, r ^ bits) for r in range(ranks)])

    def hop(value, by, sources):
        return send(by, value, "fsdp", [(2 * at + y, 2 * (at + by) + y) for at in sources for y in range(2)])

    def gather(piece, z, y, *ahead):
        got = [(piece, z * 2 + y)]

        def exchange(value, at):
            other = pair(value)
            got.extend([(value, at * 2 + y), (other, at * 2 + (y ^ 1))] if at is not z else [(other, at * 2 + (y ^ 1))])
            return other

        up1, down1 = hop(piece, 1, (0, 1, 2)), hop(piece, -1, (1, 2, 3))
        other = exchange(piece, z)
        up2, down2 = hop(after(up1, other, *ahead), 1, (1, 2)), hop(after(down1, other, *ahead), -1, (1, 2))
        other = exchange(jnp.where(z == 3, up1, down1), jnp.where(z == 3, 2, z + 1))
        up3, down3 = hop(after(up2, other), 1, (2,)), hop(after(down2, other), -1, (1,))
        exchange(jnp.where(z >= 2, up2, down2), (z + 2) % 4)
        far = jnp.where(z == 0, down3, jnp.where(z == 3, up3, up1))
        exchange(far, jnp.where(z == 0, 3, jnp.where(z == 3, 0, z - 1)))
        return got

    def gather_whole(piece):
        return lax.all_gather(piece, "fsdp", axis=0, tiled=True)

    def plus(*terms):
        total = terms[0].astype(F32)
        for term in terms[1:]:
            total = total + term.astype(F32)
        return total.astype(BF)

    def scatter_whole(value):
        return lax.psum_scatter(value, "fsdp", scatter_dimension=0, tiled=True)

    def scatter_along(value):
        lines = [[2 * at + y for at in range(ring)] for y in range(2)]
        flat = value.reshape((-1,) + value.shape[2:])
        return lax.psum_scatter(flat, "fsdp", scatter_dimension=0, tiled=True, axis_index_groups=lines)

    def gather_group(value):
        two = across(value, 2)
        return [value, across(value, 1), two, across(two, 1)]

    def scatter_group(parts):
        leaving["far"] = plus(parts[2], across(parts[3], 1))
        far = across(leaving["far"], 2)
        return parts[0], across(parts[1], 1), far

    def by_rank(pieces, rank):
        low, high = rank % 2 == 1, rank // 2 == 1
        a, b, c, d = pieces
        a, b, c, d = (jnp.where(low, *p) for p in ((b, a), (a, b), (d, c), (c, d)))
        return [jnp.where(high, *p) for p in ((c, a), (d, b), (a, c), (b, d))]

    def on_device(
        tokens, seq_lengths, attn_gain, w_query, w_key, w_value, w_outgate, w_alpha, w_beta, conv_weight,
        decay_log, decay_bias, head_gain, w_output, mlp_gain, w_gate, w_up, w_down, cotangent,
    ):
        rows, model = tokens.shape
        heads = decay_log.shape[0]
        heads_local = heads // ranks
        width = model // ranks
        piece_rows = w_query.shape[0]
        hidden_piece = w_down.shape[0] // ranks
        hidden_cols = shards * hidden_piece
        taps_count = conv_weight.shape[0]
        buffers = ranks
        group = buffers * rows
        rank = lax.axis_index("replica")
        place = lax.axis_index("fsdp")
        z, y = place // 2, place % 2

        def owner(dz, dy):
            return ((z + dz) % ring) * 2 + (y ^ dy)

        own = lambda w: lax.dynamic_slice_in_dim(w, rank * width, width, axis=1)

        conv_parts = conv_weight.shape[1] // piece_rows
        conv_cols = conv_weight.T.reshape(conv_parts, piece_rows, taps_count)
        conv_cols = jnp.swapaxes(conv_cols, 0, 1).reshape(piece_rows, conv_parts * taps_count)
        small = jnp.concatenate([w_alpha, w_beta, attn_gain[:, None], mlp_gain[:, None], conv_cols], axis=1)
        small = jnp.pad(small, ((0, 0), (0, 128 - small.shape[1])))
        shard_in = jnp.concatenate([own(w_query), own(w_key), own(w_value), own(w_outgate), small, own(w_output)], axis=1)
        hidden = lambda w: lax.dynamic_index_in_dim(
            w.reshape(piece_rows, shards, ranks, hidden_piece), rank, 2, keepdims=False
        ).reshape(piece_rows, hidden_cols)
        shard_gu = jnp.concatenate([hidden(w_gate), hidden(w_up)], axis=1)
        shard_d = lax.dynamic_slice_in_dim(w_down, rank * hidden_piece, hidden_piece, axis=0)

        live = (jnp.arange(rows, dtype=jnp.int32) < jnp.sum(seq_lengths[0])).astype(F32)[:, None]
        note = jnp.pad(seq_lengths.astype(BF), ((0, 15), (0, model - seq_lengths.shape[1])))
        tokens_noted = jnp.concatenate([tokens, note], axis=0)
        upstream_own = cotangent * live.astype(BF)

        token_slots = gather_group(tokens_noted)
        whole_in = gather_whole(shard_in)
        upstream_slots = gather_group(upstream_own)
        lengths = jnp.stack([t[rows, : seq_lengths.shape[1]] for t in token_slots]).astype(jnp.int32)
        if by_line:
            got_d = [(piece, f * hidden_piece) for piece, f in gather(shard_d, z, y, token_slots[2])]
        else:
            got_d = [(gather_whole(shard_d), 0)]
        ahead = [*token_slots[1:], *upstream_slots[1:], *[piece for piece, _ in got_d[1:]]]
        whole_gu = gather_whole(after(shard_gu, whole_in, *ahead))

        in_cols = 4 * width + 128
        full_in = Pieces([(whole_in, 0)], model, 0, in_cols)
        full_out = Pieces([(whole_in, 0)], model, in_cols, width)
        full_gu = Pieces([(whole_gu, 0)], model)
        full_down = Pieces(got_d, hidden_cols)

        info = [rank, y]
        by_slot = lambda cols: pl.BlockSpec((rows, cols), lambda i, info: (i ^ info[0], 0))
        by_row = lambda cols: pl.BlockSpec((rows, cols), lambda i, info: (i, 0))
        a_row = pl.BlockSpec((1, 1, rows), lambda i, info: (i, 0, 0))
        lanes_of = lambda info, j: pl.ds(pl.multiple_of((info[0] ^ j) * width, 128), width)
        own_lanes = lambda info: lanes_of(info, 0)
        gain_rows = 16
        split = 2 if by_line else 1
        kept_cols = model // split

        def write_split(info, value_ref, refs):
            if not by_line:
                refs[0][...] = value_ref[...]
                return
            for other, ref in enumerate(refs):
                for at in range(ring):
                    first = (2 * at + (info[1] ^ other)) * piece_rows
                    ref[:, at * piece_rows : (at + 1) * piece_rows] = value_ref[:, pl.ds(pl.multiple_of(first, 128), piece_rows)]


        def enter_body(info, ins, weights, outs, extra):
            (w_ref,) = weights
            x_refs = ins
            pre_ref, x_own_ref, lane_ref = outs[0], outs[1 + split], outs[2 + split]
            x_ref, normed_ref = extra
            step = pl.program_id(0)

            @pl.when(step == 0)
            def _():
                picked = lax.broadcasted_iota(jnp.int32, (gain_rows, 128), 0) + 2 * heads
                picked = (picked == lax.broadcasted_iota(jnp.int32, (gain_rows, 128), 1)).astype(BF)
                for first in range(0, model, 256):
                    block = w_ref[first : first + 256, 4 * width :]
                    lane_ref[:, first : first + 256] = dot(picked, block, NT)

            for j in range(len(x_refs)):
                @pl.when(step == j)
                def _():
                    x_ref[...] = x_refs[j][:rows]

            x_own_ref[...] = x_ref[:, own_lanes(info)]
            x = x_ref[...].astype(F32)
            scale = lax.rsqrt(jnp.mean(x * x, axis=1, keepdims=True) + EPS)
            normed = (x * scale * lane_ref[0:1]).astype(BF)
            normed_ref[...] = normed
            write_split(info, normed_ref, outs[1 : 1 + split])
            pre_ref[...] = dot(normed, w_ref[...])

        slot = pl.BlockSpec((rows, model), lambda i, info: (0, 0))
        entered = []
        for first in (0, 2):
            some = lambda cols: pl.BlockSpec((rows, cols), lambda i, info: ((i + info[2]) ^ info[0], 0))
            entered.append(kernel_call(
                enter_body, "enter", 11, (2,), [rank, y, first],
                [(x, whole(x)) for x in token_slots[first : first + 2]], [full_in],
                [
                    ((group, in_cols), F32, some(in_cols)), *[((group, kept_cols), BF, some(kept_cols))] * split,
                    ((group, width), BF, some(width)),
                    ((gain_rows, model), F32, pl.BlockSpec((gain_rows, model), lambda i, info: (0, 0))),
                ],
                [pltpu.VMEM((rows, model), BF)] * 2, entered[0][: 2 + split] if entered else (),
            ))
        pre, normed, x_cols = entered[1][0], entered[1][1 : 1 + split], entered[1][1 + split]
        lanes = entered[0][2 + split]
        gain_one = lanes[0]
        own_gain = pl.BlockSpec((1, width), lambda i, info: (0, 0))
        gain_two = lax.dynamic_slice_in_dim(lanes[1:2], rank * width, width, axis=1)
        conv_all = lanes[2 : 2 + conv_parts * taps_count].reshape(conv_parts, taps_count, shards, piece_rows)
        conv_all = conv_all.transpose(1, 2, 0, 3).reshape(taps_count, 3, model)
        taps = lax.dynamic_slice_in_dim(conv_all, rank * width, width, axis=2).reshape(taps_count, 3 * width)

        rank_arr = rank[None].astype(jnp.int32)
        made = ()
        for at in range(buffers):
            source = entered[at // 2][0]
            if at == 2:
                source = pre
            made = mixer_forward(
                at, rank_arr, lengths, decay_log, decay_bias, source, taps, head_gain[None], heads_local, made
            )
        gated, inverse = made

        def leave_body(info, ins, weights, outs, extra):
            (w_ref,) = weights
            x_ref, gain_ref = ins[ranks:]
            resid_ref, branch_ref, scaled_ref, square_ref = outs[split:]
            (all_ref,) = extra
            for j in range(ranks):
                all_ref[:, lanes_of(info, j)] = ins[j][...]
            write_split(info, all_ref, outs[:split])
            branch = dot(all_ref[...], w_ref[...])
            resid = x_ref[...].astype(F32) + branch
            resid_ref[...] = resid
            branch_ref[...] = branch
            scaled_ref[...] = (resid * gain_ref[...]).astype(BF)
            square_ref[0] = to_row(jnp.sum(resid * resid, axis=1, keepdims=True), diagonal(rows))

        *gated_all, resid, branch, scaled, square = kernel_call(
            leave_body, "leave", 9, (buffers,), info,
            [(g, by_row(width)) for g in gather_group(gated)] + [(x_cols, by_row(width)), (gain_two, own_gain)],
            [full_out],
            [
                *[((group, kept_cols), BF, by_row(kept_cols))] * split, ((group, width), F32, by_row(width)),
                ((group, width), F32, by_row(width)), ((group, width), BF, by_row(width)),
                ((buffers, 1, rows), F32, a_row),
            ],
            [pltpu.VMEM((rows, model), BF)],
        )
        squares = gather_group(square)

        def inverse_scale(square_refs):
            total = square_refs[0][0]
            for ref in square_refs[1:]:
                total = total + ref[0]
            return lax.rsqrt(to_col(total, diagonal(rows)) / model + EPS)

        def hidden_body(info, ins, weights, outs, extra):
            w_ref, d_ref = weights
            hidden_ref, grad_ref, stat_ref, u_ref, u_own_ref = outs[split:]
            (all_ref,) = extra
            for j in range(ranks):
                @pl.when(pl.program_id(0) ^ info[0] == j)
                def _():
                    u_ref[...] = ins[2 * ranks + j][...]

            u_own_ref[...] = u_ref[:, own_lanes(info)]
            for j in range(ranks):
                all_ref[:, lanes_of(info, j)] = ins[j][...]
            write_split(info, all_ref, outs[:split])
            inv = inverse_scale(ins[ranks : 2 * ranks])
            raw_gate = dot(all_ref[...], w_ref[:, :hidden_cols])
            raw_up = dot(all_ref[...], w_ref[:, hidden_cols:])
            grad_hidden = dot(u_ref[...], d_ref[...], NT)
            gate, up = raw_gate * inv, raw_up * inv
            sig = jax.nn.sigmoid(gate)
            opened = gate * sig
            hidden_ref[...] = (opened * up).astype(BF)
            grad_hidden = grad_hidden * inv
            grad_gate = (grad_hidden * up * (sig * (1.0 + gate * (1.0 - sig)))).astype(BF)
            grad_up = (grad_hidden * opened).astype(BF)
            grad_ref[:, :hidden_cols] = grad_gate
            grad_ref[:, hidden_cols:] = grad_up
            stat = jnp.sum(raw_gate * grad_gate.astype(F32) + raw_up * grad_up.astype(F32), axis=1, keepdims=True)
            stat_ref[0] = to_row(stat, diagonal(rows))

        *scaled_all, hidden_b, grad_gu, stat, upstream, u_cols = kernel_call(
            hidden_body, "hidden", 33, (buffers,), info,
            [(s, by_row(width)) for s in gather_group(scaled)] + [(s, a_row) for s in squares]
            + [(u, slot) for u in upstream_slots],
            [full_gu, full_down],
            [
                *[((group, kept_cols), BF, by_row(kept_cols))] * split, ((group, hidden_cols), BF, by_row(hidden_cols)),
                ((group, 2 * hidden_cols), BF, by_row(2 * hidden_cols)), ((buffers, 1, rows), F32, a_row),
                ((group, model), BF, by_row(model)), ((group, width), BF, by_row(width)),
            ],
            [pltpu.VMEM((rows, model), BF)],
        )
        stats = gather_group(stat)

        def back_body(info, ins, weights, outs, extra):
            for j in range(ranks):
                outs[j][...] = dot(ins[0][...], weights[0][lanes_of(info, j)], NT).astype(BF)

        def scattered(lefts, right, piece, *begin):
            if not by_line:
                value = dot(lefts[0], right, TN).astype(BF)
                return value, lambda *events: (scatter_whole(value), value)
            kept, sent = (dot(left, right, TN).astype(BF) for left in lefts)
            return exchanged(kept, sent, piece, *begin)

        def exchanged(kept, sent, piece, *begin):
            given = lax.ppermute(after(sent, *begin), "fsdp", [(f, f ^ 1) for f in range(shards)])

            def end(*events):
                total = plus(after(kept, *events), given)
                return scatter_along(total.reshape(ring, piece, -1)), total

            return sent, end

        sent_gate, end_gate = scattered(scaled_all, grad_gu[:, :hidden_cols], piece_rows)
        parts = kernel_call(
            back_body, "back", 19, (buffers,), info, [(after(grad_gu, sent_gate), by_row(2 * hidden_cols))], [full_gu],
            [((group, width), BF, by_row(width))] * ranks,
        )
        terms_two = scatter_group(parts)

        sent_up, end_up = scattered(scaled_all, grad_gu[:, hidden_cols:], piece_rows, parts[0])
        d_down = dot(hidden_b, upstream, TN).astype(BF)

        def turn_body(info, ins, weights, outs, extra):
            (w_ref,) = weights
            own_ref, near_ref, far_ref, resid_ref, u_ref, gain_ref = ins[:6]
            grad_ref, out_refs, gain_out_ref = outs[0], outs[1 : 1 + ranks], outs[1 + ranks]

            @pl.when(pl.program_id(0) == 0)
            def _():
                gain_out_ref[...] = jnp.zeros_like(gain_out_ref)

            grad_two = own_ref[...].astype(F32) + near_ref[...].astype(F32) + far_ref[...].astype(F32)
            resid = resid_ref[...]
            inv = inverse_scale(ins[6 : 6 + ranks])
            total = ins[6 + ranks][0]
            for ref in ins[7 + ranks :]:
                total = total + ref[0]
            stat = to_col(total, diagonal(rows))
            gain_out_ref[...] += jnp.sum(grad_two * resid, axis=0, keepdims=True)
            grad = u_ref[...].astype(F32) + gain_ref[...] * grad_two - resid * (inv * inv * stat / model)
            grad = grad.astype(BF)
            grad_ref[...] = grad
            for j in range(ranks):
                out_refs[j][...] = dot(grad, w_ref[lanes_of(info, j)], NT).astype(BF)

        turned = kernel_call(
            turn_body, "turn", 9, (buffers,), info,
            [(t, by_row(width)) for t in terms_two]
            + [(after(resid, d_down, sent_up), by_row(width)), (u_cols, by_row(width)), (gain_two, own_gain)]
            + [(s, a_row) for s in squares] + [(s, a_row) for s in stats],
            [full_out],
            [((group, width), BF, by_row(width))] * (1 + ranks) + [((1, width), F32, own_gain)],
        )
        grad_branch, grad_mlp_gain = turned[0], turned[1 + ranks][0]
        terms_gated = scatter_group(turned[1 : 1 + ranks])
        if by_line:
            placed = d_down.reshape(ring, 2, hidden_piece, model)
            side = lambda at: lax.dynamic_index_in_dim(placed, at, 1, keepdims=False).reshape(ring * hidden_piece, model)
            _, end_down = exchanged(side(y), side(1 - y), hidden_piece, grad_branch)
        else:
            end_down = lambda *events: (scatter_whole(d_down), d_down)
        own_block = lambda value, j: lax.dynamic_slice_in_dim(value, (rank ^ j) * rows, rows, axis=0)

        def to_tokens(value):
            pieces = [own_block(value, 0)] + [across(own_block(value, j), j) for j in range(1, ranks)]
            return jnp.concatenate(by_rank(pieces, rank), axis=1).astype(F32)

        def down_body(info, ins, weights, outs, extra):
            (full,) = extra
            full[...] = dot(ins[0][...], weights[0][...])
            full[:, own_lanes(info)] += ins[1][...]
            for j in range(ranks):
                @pl.when(pl.program_id(0) == j)
                def _():
                    outs[j][...] = full[...].astype(BF)

        down = kernel_call(
            down_body, "down", 14, (ranks,), info, [(after(hidden_b, leaving["far"]), by_slot(hidden_cols)), (branch, by_slot(width))], [full_down],
            [((rows, model), BF, slot)] * ranks, [pltpu.VMEM((rows, model), F32)],
        )
        down_terms = scatter_group(down)
        output = tokens.astype(F32)
        for term in down_terms:
            output = output + term.astype(F32)
        output = (output * live).astype(BF)
        grad_resid_own = to_tokens(grad_branch)

        made = ()
        share_gate, _ = end_gate(down[0])
        ahead = [tuple(down), (), (), (down_terms[2],)]
        for at in range(buffers):
            made = mixer_backward(
                at, rank_arr, lengths, decay_log, decay_bias, after(pre, *ahead[at]), taps, head_gain[None], inverse,
                terms_gated, heads_local, made,
            )
            if at == 0:
                _, end_out = scattered(gated_all, grad_branch, piece_rows, made[1])
            if at == 1:
                share_up, _ = end_up(made[1])
        d_pre, d_taps, d_head_gain, d_decay = made
        cuts = ((0, 2 * width), (2 * width, 2 * width + 128))
        ends_in = [scattered(normed, d_pre[:, first : first + count], piece_rows) for first, count in cuts]
        d_in = [sent for sent, _ in ends_in]
        share_d, _ = end_down(*d_in)

        def first_body(info, ins, weights, outs, extra):
            result = dot(ins[0][...], weights[0][...], NT).astype(BF)
            for j in range(ranks):
                @pl.when(pl.program_id(0) == j)
                def _():
                    outs[j][...] = result

        grad_slots = kernel_call(
            first_body, "first", 19, (ranks,), info, [(after(d_pre, *d_in), by_slot(in_cols))], [full_in],
            [((rows, model), BF, slot)] * ranks,
        )
        first_terms = scatter_group(grad_slots)
        grad_one = sum(t.astype(F32) for t in first_terms)
        share_o, sum_o = end_out(grad_slots[0])
        share_a, sum_a = ends_in[0][1](sum_o, first_terms[2])
        share_b, sum_b = ends_in[1][1](sum_a)
        x_own = tokens.astype(F32)
        inv_one = lax.rsqrt(jnp.mean(x_own * x_own, axis=-1, keepdims=True) + EPS)
        grad_attn_gain = jnp.sum(grad_one * x_own * inv_one, axis=0)
        pulled = gain_one * grad_one
        grad_x = inv_one * pulled - x_own * (inv_one**3 * jnp.mean(pulled * x_own, axis=-1, keepdims=True))
        grad_tokens = (grad_resid_own + grad_x).astype(BF)

        def finish_body(info, ins, weights, outs, extra):
            for j in range(ranks):
                for at, out in enumerate(outs):
                    out[:, lanes_of(info, j)] = ins[j][:, at * width : (at + 1) * width].astype(F32)

        def finish(slots, count):
            tile = piece_rows // 4
            tiled = lambda cols: pl.BlockSpec((tile, cols), lambda i, info: (i, 0))
            return kernel_call(
                finish_body, "finish", 5, (4,), info, [(v, tiled(v.shape[1])) for v in slots], [],
                [((piece_rows, model), F32, tiled(model))] * count,
            )

        def unhide_body(info, ins, weights, outs, extra):
            (held,) = extra
            for j in range(ranks):
                held[info[0] ^ j] = ins[j][...]
            for out in outs:
                for f in range(shards):
                    first = f * hidden_piece
                    out[:, f * ranks * hidden_piece : (f + 1) * ranks * hidden_piece] = jnp.concatenate(
                        [held[b, :, first : first + hidden_piece].astype(F32) for b in range(ranks)], axis=1
                    )

        def unhide(slots):
            tile = piece_rows // 4
            tiled = lambda cols: pl.BlockSpec((tile, cols), lambda i, info: (i, 0))
            full = shards * ranks * hidden_piece
            [result] = kernel_call(
                unhide_body, "unhide", 8, (4,), info, [(v, tiled(v.shape[1])) for v in slots], [],
                [((piece_rows, full), F32, tiled(full))], [pltpu.VMEM((ranks, tile, hidden_cols), BF)],
            )
            return result

        own_cols = lambda value: lax.dynamic_update_slice_in_dim(
            jnp.zeros(value.shape[:-1] + (model,), F32), value, rank * width, axis=value.ndim - 1
        )
        packed = jnp.concatenate(
            [
                own_cols(d_taps.reshape(taps_count, 3, width)).reshape(-1),
                own_cols(grad_mlp_gain),
                grad_attn_gain,
                d_head_gain[0],
                d_decay[0, :heads],
                d_decay[1, :heads],
            ]
        )
        total = jnp.pad(packed, (0, -packed.size % 1024)).reshape(-1, 128)
        for bits in (1, 2):
            total = total + lax.ppermute(total, "replica", [(r, r ^ bits) for r in range(ranks)])
        bits = 1
        while bits < shards:
            total = total + lax.ppermute(total, "fsdp", [(f, f ^ bits) for f in range(shards)])
            bits *= 2
        total = total.reshape(-1)
        conv_size = taps_count * 3 * model
        sum_conv = total[:conv_size].reshape(taps_count, shards, -1)
        sum_conv = lax.dynamic_index_in_dim(sum_conv, place, 1, keepdims=False)
        at = conv_size
        sum_mlp_gain = lax.dynamic_slice_in_dim(total, at + place * piece_rows, piece_rows)
        sum_attn_gain = lax.dynamic_slice_in_dim(total, at + model + place * piece_rows, piece_rows)
        at += 2 * model
        sum_head_gain = total[at : at + head_gain.size]
        at += head_gain.size
        sum_log, sum_bias = total[at : at + heads], total[at + heads : at + 2 * heads]

        gate_slots, up_slots = gather_group(share_gate), gather_group(share_up)
        out_gate = unhide(gate_slots)
        d_slots = gather_group(after(share_d, out_gate))
        out_up = unhide(up_slots)
        o_slots = gather_group(after(share_o, out_up))
        out_down = jnp.concatenate(by_rank(d_slots, rank), axis=0).astype(F32)
        a_slots = gather_group(after(share_a, out_down))
        [out_output] = finish(o_slots, 1)
        out_query, out_key = finish(a_slots, 2)
        finished = (out_gate, out_up, out_down, out_output, output, grad_tokens, sum_conv, out_query, out_key)
        share_b, *finished = lax.optimization_barrier((share_b, *finished))
        out_gate, out_up, out_down, out_output, output, grad_tokens, sum_conv, out_query, out_key = finished
        b_slots = gather_group(share_b)
        out_value, out_outgate = finish(b_slots, 2)
        low = [p[:, 2 * width :].astype(F32) for p in b_slots]
        low = (low[0] + low[1]) + (low[2] + low[3])
        out_alpha, out_beta = low[:, :heads], low[:, heads : 2 * heads]
        return (
            output, grad_tokens, sum_attn_gain, out_query, out_key, out_value, out_outgate, out_alpha, out_beta,
            sum_conv, sum_log, sum_bias, sum_head_gain, out_output, sum_mlp_gain, out_gate, out_up, out_down,
        )

    return on_device


def solution(mesh):
    rows, cols = P("fsdp", None), P("fsdp")
    tokens = P(("replica", "fsdp"), None)
    return jax.shard_map(
        program(mesh.shape["fsdp"], mesh.shape["replica"]),
        mesh=mesh,
        in_specs=(
            tokens, tokens, cols, rows, rows, rows, rows, rows, rows, P(None, "fsdp"), P(), P(), P(), rows, cols,
            rows, rows, rows, tokens,
        ),
        out_specs=(
            tokens, tokens, cols, rows, rows, rows, rows, rows, rows, P(None, "fsdp"), P(), P(), P(), rows, cols,
            rows, rows, rows,
        ),
        check_vma=False,
    )
```

```python
import copy
from functools import partial

import jax
import jax.numpy as jnp
import numpy as np
from jax import lax
from jax.experimental import pallas as pl
from jax.experimental.pallas import tpu as pltpu
from jax.sharding import PartitionSpec as P

EPS = 1e-06
BF = jnp.bfloat16
F32 = jnp.float32
NN = (((1,), (0,)), ((), ()))
NT = (((1,), (1,)), ((), ()))
TN = (((0,), (0,)), ((), ()))


def one_pass(left, right, dims=NN):
    return lax.dot_general(left.astype(BF), right.astype(BF), dims, preferred_element_type=F32)


def halves(value):
    high = value.astype(BF)
    return high, (value - high.astype(F32)).astype(BF)


def three_pass(left, right, dims=NN):
    lh, ll = left if isinstance(left, tuple) else halves(left)
    rh, rl = right if isinstance(right, tuple) else halves(right)
    total = lax.dot_general(lh, rh, dims, preferred_element_type=F32)
    total = total + lax.dot_general(lh, rl, dims, preferred_element_type=F32)
    return total + lax.dot_general(ll, rh, dims, preferred_element_type=F32)


def layout(length_of, count, rows):
    col = lax.broadcasted_iota(jnp.int32, (rows, 1), 0)
    row = lax.broadcasted_iota(jnp.int32, (1, rows), 1)
    bound = jnp.int32(0)
    start_col = jnp.zeros_like(col)
    start_row = jnp.zeros_like(row)
    for at in range(count):
        bound = bound + length_of(at)
        start_col = jnp.where(col >= bound, bound, start_col)
        start_row = jnp.where(row >= bound, bound, start_row)
    same = start_col == start_row
    within = same & (col >= row)
    strict = same & (col > row)
    return col, row, col - start_col, within, strict


def conv_sum(pre, taps, offset):
    total = pre * taps[0:1]
    for by in range(1, taps.shape[0]):
        moved = jnp.where(offset >= by, pltpu.roll(pre, by, 0), 0.0)
        total = total + moved * taps[by : by + 1]
    return total


def to_row(column, eye):
    return jnp.sum(jnp.where(eye, column, 0.0), axis=0, keepdims=True)


def lane_of(block, lane):
    lanes = lax.broadcasted_iota(jnp.int32, block.shape, 1)
    return jnp.sum(jnp.where(lanes == lane, block, 0.0), axis=1, keepdims=True)


def softplus(value):
    return jnp.maximum(value, 0.0) + jnp.log1p(jnp.exp(-jnp.abs(value)))


def head_parts(pre_ref, taps_ref, small, head, local, heads_local, head_size, heads_all, decay_log, decay_bias, geo):
    col, row, offset, within, strict, eye = geo
    width = heads_local * head_size
    at = lambda part: slice(part * width + local * head_size, part * width + (local + 1) * head_size)
    pres = [pre_ref[:, at(part)] for part in range(3)]
    taps = [taps_ref[:, at(part)] for part in range(3)]
    sums = [conv_sum(p, t, offset) for p, t in zip(pres, taps)]
    sigs = [jax.nn.sigmoid(s) for s in sums]
    convs = [s * g for s, g in zip(sums, sigs)]
    scale_q = lax.rsqrt(jnp.sum(convs[0] * convs[0], axis=1, keepdims=True) + EPS)
    scale_k = lax.rsqrt(jnp.sum(convs[1] * convs[1], axis=1, keepdims=True) + EPS)
    query = (convs[0] * scale_q * head_size**-0.5).astype(BF)
    key = (convs[1] * scale_k).astype(BF)
    value = convs[2].astype(BF)
    shifted = lane_of(small, head) + decay_bias
    beta = jax.nn.sigmoid(lane_of(small, heads_all + head))
    rate = -jnp.exp(jnp.full_like(shifted, decay_log))
    decay = rate * softplus(shifted)
    reach = jnp.where(within, to_row(decay, eye), 0.0)
    total_col = jnp.sum(reach, axis=1, keepdims=True)
    total_row = to_row(total_col, eye)
    fall = jnp.where(within, jnp.exp(jnp.where(within, total_col - total_row, 0.0)), 0.0)
    fall_strict = jnp.where(strict, fall, 0.0)
    keys = lax.dot_general(key, key, NT, preferred_element_type=F32)
    scores = lax.dot_general(query, key, NT, preferred_element_type=F32)
    return dict(pres=pres, taps=taps, sums=sums, sigs=sigs, convs=convs, scale_q=scale_q, scale_k=scale_k,
                query=query, key=key, value=value, shifted=shifted, beta=beta, rate=rate, decay=decay,
                fall=fall, fall_strict=fall_strict, keys=keys, scores=scores,
                gate=pre_ref[:, at(3)])


def two_pass(left, right, dims=NN):
    high, low = halves(left)
    return lax.dot_general(high, right, dims, preferred_element_type=F32) + lax.dot_general(
        low, right, dims, preferred_element_type=F32
    )


def unit_inverses(lowers):
    half = lowers[0].shape[0] // 2
    col = lax.broadcasted_iota(jnp.int32, (half, half), 0)
    row = lax.broadcasted_iota(jnp.int32, (half, half), 1)
    both = jnp.where(col > row, col ^ row, 0)
    eye = (col == row).astype(F32)
    blocks = [low[at : at + half, at : at + half] for low in lowers for at in (0, half)]
    inverses = [eye - jnp.where(both == 1, block, 0.0) for block in blocks]
    reach = 2
    while reach < half:
        corner = (both >= reach) & (both < 2 * reach)
        small = [inverse.astype(BF) for inverse in inverses]
        steps = [one_pass(jnp.where(corner, block, 0.0), inverse) for block, inverse in zip(blocks, small)]
        inverses = [inverse - one_pass(s, step) for inverse, s, step in zip(inverses, small, steps)]
        reach *= 2
    small = [inverse.astype(BF) for inverse in inverses]
    steps = [one_pass(low[half:, :half], small[2 * at]) for at, low in enumerate(lowers)]
    corners = [one_pass(small[2 * at + 1], step) for at, step in enumerate(steps)]
    zero = jnp.zeros((half, half), BF)
    return [
        jnp.concatenate(
            [
                jnp.concatenate([small[2 * at], zero], axis=1),
                jnp.concatenate([(-corner).astype(BF), small[2 * at + 1]], axis=1),
            ],
            axis=0,
        )
        for at, corner in enumerate(corners)
    ]


def solve_all(lowers, inverses, rights, dims=NN):
    results = [one_pass(inverse, right, dims) for inverse, right in zip(inverses, rights)]
    lefts = [
        right - result - three_pass(lower, result, dims) for lower, right, result in zip(lowers, rights, results)
    ]
    return [result + one_pass(inverse, left, dims) for result, inverse, left in zip(results, inverses, lefts)]


def forward_kernel(cfg, step, rank_ref, len_ref, log_ref, bias_ref, pre_ref, taps_ref, gain_ref, *refs):
    heads_local, head_size, heads_all, dot_use = cfg
    rows = pre_ref.shape[0]
    gated_ref, inv_ref = refs[-2:]
    col, row, offset, within, strict = layout(lambda at: len_ref[step, at], len_ref.shape[1], rows)
    eye = col == row
    geo = (col, row, offset, within, strict, eye)
    small = pre_ref[:, 4 * heads_local * head_size :]
    parts = []
    for local in range(heads_local):
        head = rank_ref[0] * heads_local + local
        parts.append(head_parts(pre_ref, taps_ref, small, head, local, heads_local, head_size, heads_all, log_ref[head], bias_ref[head], geo))
    lowers = [p["beta"] * p["fall_strict"] * p["keys"] for p in parts]
    inverses = unit_inverses(lowers)
    updates = solve_all(lowers, inverses, [p["beta"] * p["value"].astype(F32) for p in parts])
    mixeds = [dot_use(p["scores"] * p["fall"], update) for p, update in zip(parts, updates)]
    for local, (p, inverse, mixed) in enumerate(zip(parts, inverses, mixeds)):
        inv_ref[0, local] = inverse
        scale = lax.rsqrt(jnp.mean(mixed * mixed, axis=1, keepdims=True) + EPS)
        gate = p["gate"]
        out = mixed * scale * gain_ref[...] * (gate * jax.nn.sigmoid(gate))
        gated_ref[:, local * head_size : (local + 1) * head_size] = out.astype(BF)


def backward_kernel(cfg, step, rank_ref, len_ref, log_ref, bias_ref, pre_ref, taps_ref, gain_ref, inv_ref, own_ref, near_ref, far_ref, *refs):
    heads_local, head_size, heads_all, dot_use = cfg
    rows = pre_ref.shape[0]
    dpre_ref, dtaps_ref, dgain_ref, ddecay_ref = refs[-4:]
    for sum_ref, at in zip((dtaps_ref, dgain_ref, ddecay_ref), range(1, 4)):
        sum_ref[...] = refs[at][...] if step else jnp.zeros_like(sum_ref)

    col, row, offset, within, strict = layout(lambda at: len_ref[step, at], len_ref.shape[1], rows)
    eye = col == row
    geo = (col, row, offset, within, strict, eye)
    width = heads_local * head_size
    small = pre_ref[:, 4 * width :]
    dsmall = jnp.zeros_like(small)
    lanes = lax.broadcasted_iota(jnp.int32, small.shape, 1)
    row_lanes = lax.broadcasted_iota(jnp.int32, (1, ddecay_ref.shape[1]), 1)
    everyone = range(heads_local)
    heads = [rank_ref[0] * heads_local + local for local in everyone]
    at = lambda part, local: slice(part * width + local * head_size, part * width + (local + 1) * head_size)
    ps = [
        head_parts(pre_ref, taps_ref, small, head, local, heads_local, head_size, heads_all, log_ref[head], bias_ref[head], geo)
        for local, head in zip(everyone, heads)
    ]
    gain = gain_ref[...]
    betas = [p["beta"] for p in ps]
    values = [p["value"].astype(F32) for p in ps]
    inverses = [inv_ref[0, local] for local in everyone]
    spreads = [p["fall_strict"] * p["keys"] for p in ps]
    lowers = [beta * spread for beta, spread in zip(betas, spreads)]
    attns = [p["scores"] * p["fall"] for p in ps]
    updates = solve_all(lowers, inverses, [beta * value for beta, value in zip(betas, values)])
    mixeds = [dot_use(attn, update) for attn, update in zip(attns, updates)]
    dmixeds = []
    for local, (p, mixed) in enumerate(zip(ps, mixeds)):
        lanes_of = slice(local * head_size, (local + 1) * head_size)
        grad = own_ref[:, lanes_of].astype(F32) + near_ref[:, lanes_of].astype(F32) + far_ref[:, lanes_of].astype(F32)
        gate = p["gate"]
        sig = jax.nn.sigmoid(gate)
        opened = gate * sig
        scale = lax.rsqrt(jnp.mean(mixed * mixed, axis=1, keepdims=True) + EPS)
        normed = mixed * scale
        dpre_ref[:, at(3, local)] = (grad * normed * gain * (sig * (1.0 + gate * (1.0 - sig)))).astype(BF)
        dgain_ref[...] += jnp.sum(grad * opened * normed, axis=0, keepdims=True)
        dnormed = grad * opened * gain
        dmixeds.append(scale * (dnormed - normed * jnp.mean(dnormed * normed, axis=1, keepdims=True)))
    dupdates = [dot_use(attn, dmixed, TN) for attn, dmixed in zip(attns, dmixeds)]
    dattns = [jnp.where(within, dot_use(dmixed, update, NT), 0.0) for dmixed, update in zip(dmixeds, updates)]
    drights = solve_all(lowers, inverses, dupdates, TN)
    dlowers = [jnp.where(strict, -dot_use(dright, update, NT), 0.0) for dright, update in zip(drights, updates)]
    dscores = [dattn * p["fall"] for dattn, p in zip(dattns, ps)]
    dkeys = [dlower * beta * p["fall_strict"] for dlower, beta, p in zip(dlowers, betas, ps)]
    dqueries = [two_pass(dscore, p["key"]) for dscore, p in zip(dscores, ps)]
    dkey_rows = [
        two_pass(dscore, p["query"], TN) + two_pass(dkey, p["key"]) + two_pass(dkey, p["key"], TN)
        for dscore, dkey, p in zip(dscores, dkeys, ps)
    ]
    later = (col <= row) & (col - offset == row_start(row, len_ref, step))
    for local, (head, p) in enumerate(zip(heads, ps)):
        beta, dright, dlower, dattn = betas[local], drights[local], dlowers[local], dattns[local]
        dbeta = jnp.sum(dright * values[local], axis=1, keepdims=True)
        dbeta = dbeta + jnp.sum(dlower * spreads[local], axis=1, keepdims=True)
        pairs = dattn * attns[local] + dlower * lowers[local]
        dtotal_row = to_row(jnp.sum(pairs, axis=1, keepdims=True), eye) - jnp.sum(pairs, axis=0, keepdims=True)
        ddecay = jnp.sum(jnp.where(later, dtotal_row, 0.0), axis=1, keepdims=True)
        dshifted = ddecay * p["rate"] * jax.nn.sigmoid(p["shifted"])
        dlog = jnp.sum(ddecay * p["decay"], axis=0, keepdims=True)
        dbias = jnp.sum(dshifted, axis=0, keepdims=True)
        ddecay_ref[0:1] += jnp.where(row_lanes == head, dlog, 0.0)
        ddecay_ref[1:2] += jnp.where(row_lanes == head, dbias, 0.0)
        dsmall = dsmall + jnp.where(lanes == head, dshifted, 0.0)
        dsmall = dsmall + jnp.where(lanes == heads_all + head, dbeta * beta * (1.0 - beta), 0.0)
        rounded = [g.astype(BF).astype(F32) for g in (dqueries[local], dkey_rows[local], beta * dright)]
        cq, ck = p["convs"][0], p["convs"][1]
        gq = rounded[0] * head_size**-0.5
        dconvs = [
            p["scale_q"] * (gq - cq * (p["scale_q"] * p["scale_q"] * jnp.sum(gq * cq, axis=1, keepdims=True))),
            p["scale_k"] * (rounded[1] - ck * (p["scale_k"] * p["scale_k"] * jnp.sum(rounded[1] * ck, axis=1, keepdims=True))),
            rounded[2],
        ]
        for part in range(3):
            sig_c, total, taps, pre = p["sigs"][part], p["sums"][part], p["taps"][part], p["pres"][part]
            dsum = dconvs[part] * (sig_c * (1.0 + total * (1.0 - sig_c)))
            dpre = dsum * taps[0:1]
            dtaps_ref[0:1, at(part, local)] += jnp.sum(dsum * pre, axis=0, keepdims=True)
            for by in range(1, taps.shape[0]):
                kept = jnp.where(offset >= by, dsum, 0.0)
                dtaps_ref[by : by + 1, at(part, local)] += jnp.sum(kept * pltpu.roll(pre, by, 0), axis=0, keepdims=True)
                dpre = dpre + pltpu.roll(kept, rows - by, 0) * taps[by : by + 1]
            dpre_ref[:, at(part, local)] = dpre.astype(BF)
    dpre_ref[:, 4 * width :] = dsmall.astype(BF)


def row_start(row, len_ref, step):
    bound = jnp.int32(0)
    start = jnp.zeros_like(row)
    for at in range(len_ref.shape[1]):
        bound = bound + len_ref[step, at]
        start = jnp.where(row >= bound, bound, start)
    return start


def mixer_forward(at, rank, lengths, decay_log, decay_bias, pre, taps, gain, heads_local, made):
    buffers = lengths.shape[0]
    rows = pre.shape[0] // buffers
    head_size = gain.shape[1]
    cfg = (heads_local, head_size, decay_log.shape[0], three_pass)
    smem = pl.BlockSpec(memory_space=pltpu.SMEM)
    entire = lambda a: pl.BlockSpec(a.shape, lambda i, rank: (0,) * a.ndim)
    by_rows = lambda cols: pl.BlockSpec((rows, cols), lambda i, rank: (at ^ rank[0], 0))
    width = heads_local * head_size
    return pl.pallas_call(
        partial(forward_kernel, cfg, at),
        grid_spec=pltpu.PrefetchScalarGridSpec(
            num_scalar_prefetch=1,
            grid=(1,),
            in_specs=[smem, smem, smem, by_rows(pre.shape[1]), entire(taps), entire(gain)]
            + [pl.BlockSpec(memory_space=pl.ANY)] * len(made),
            out_specs=[by_rows(width), pl.BlockSpec((1, heads_local, rows, rows), lambda i, rank: (at ^ rank[0], 0, 0, 0))],
        ),
        out_shape=[jax.ShapeDtypeStruct((buffers * rows, width), BF),
                   jax.ShapeDtypeStruct((buffers, heads_local, rows, rows), BF)],
        input_output_aliases={7 + n: n for n in range(len(made))},
        compiler_params=pltpu.CompilerParams(vmem_limit_bytes=48 << 20),
        cost_estimate=pl.CostEstimate(flops=int(19e6), bytes_accessed=1 << 10, transcendentals=0),
        name="mixer_forward",
    )(rank, lengths, decay_log, decay_bias, pre, taps, gain, *made)


def mixer_backward(at, rank, lengths, decay_log, decay_bias, pre, taps, gain, inverse, grads, heads_local, made):
    buffers = lengths.shape[0]
    rows = pre.shape[0] // buffers
    head_size = gain.shape[1]
    cfg = (heads_local, head_size, decay_log.shape[0], three_pass)
    smem = pl.BlockSpec(memory_space=pltpu.SMEM)
    entire = lambda s: pl.BlockSpec(s, lambda i, rank: (0,) * len(s))
    by_rows = lambda a: pl.BlockSpec((rows, a.shape[1]), lambda i, rank: (at ^ rank[0], 0))
    sums = [entire(taps.shape), entire(gain.shape), entire((8, 128))]
    return pl.pallas_call(
        partial(backward_kernel, cfg, at),
        grid_spec=pltpu.PrefetchScalarGridSpec(
            num_scalar_prefetch=1,
            grid=(1,),
            in_specs=[smem, smem, smem, by_rows(pre), entire(taps.shape), entire(gain.shape),
                      pl.BlockSpec((1, heads_local, rows, rows), lambda i, rank: (at ^ rank[0], 0, 0, 0)),
                      *[by_rows(g) for g in grads]]
            + ([pl.BlockSpec(memory_space=pl.ANY)] + sums if made else []),
            out_specs=[by_rows(pre)] + sums,
        ),
        out_shape=[jax.ShapeDtypeStruct(pre.shape, BF), jax.ShapeDtypeStruct(taps.shape, F32),
                   jax.ShapeDtypeStruct(gain.shape, F32), jax.ShapeDtypeStruct((8, 128), F32)],
        input_output_aliases={11: 0} if made else {},
        compiler_params=pltpu.CompilerParams(vmem_limit_bytes=48 << 20),
        cost_estimate=pl.CostEstimate(flops=int(12e6), bytes_accessed=1 << 10, transcendentals=0),
        name="mixer_backward",
    )(rank, lengths, decay_log, decay_bias, pre, taps, gain, inverse, *grads, *made)


def dot(left, right, dims=NN):
    return lax.dot_general(left, right, dims, preferred_element_type=F32)


ANY = pl.BlockSpec(memory_space=pl.ANY)
LIMIT = 56 << 20
INV, OWN, RANK = 0, 1, 2


def whole(array):
    return pl.BlockSpec(array.shape, lambda i, info: (0,) * array.ndim)


def to_col(row, eye):
    return jnp.sum(jnp.where(eye, row, 0.0), axis=1, keepdims=True)


def diagonal(rows):
    return lax.broadcasted_iota(jnp.int32, (rows, rows), 0) == lax.broadcasted_iota(jnp.int32, (rows, rows), 1)


class Pieces:
    def __init__(self, parts, rows, first=0, columns=None):
        self.arrays, self.starts = [a for a, _ in parts], [jnp.asarray(s, jnp.int32) for _, s in parts]
        self.first, self.shape = first, (rows, columns or parts[0][0].shape[1])

    def copies(self, info, base, sources, target, sem, sem_base):
        made = []
        for at, source in enumerate(sources):
            rows, cols = source.shape[0], self.shape[1]
            source = source.at[:, pl.ds(self.first, cols)]
            place = target.at[pl.ds(pl.multiple_of(info[base + at], 16), rows)]
            made.append(pltpu.make_async_copy(source, place, sem.at[sem_base + at]))
        return made


def kernel_call(body, name, cost, grid, info, ins, weights, outs, scratch=(), onto=()):
    lead = len(info)
    scalars = jnp.stack([jnp.asarray(v, jnp.int32) for v in info] + [s for w in weights for s in w.starts])
    counts = [len(w.arrays) for w in weights]
    total = sum(counts)

    def kernel(info_ref, *refs):
        in_refs, refs = refs[: len(ins)], refs[len(ins) :]
        piece_refs, refs = refs[:total], refs[total:]
        refs = refs[len(onto) :]
        out_refs, refs = refs[: len(outs)], refs[len(outs) :]
        full_refs, refs = refs[: len(weights)], refs[len(weights) :]
        extra = refs[: len(scratch)]
        if total:
            sem = refs[len(scratch)]

            @pl.when(pl.program_id(0) == 0)
            def _():
                made, at = [], 0
                for w, full, count in zip(weights, full_refs, counts):
                    made += w.copies(info_ref, lead + at, piece_refs[at : at + count], full, sem, at)
                    at += count
                for move in made:
                    move.start()
                for move in made:
                    move.wait()

        body(info_ref, in_refs, full_refs, out_refs, extra)

    return pl.pallas_call(
        kernel,
        grid_spec=pltpu.PrefetchScalarGridSpec(
            num_scalar_prefetch=1,
            grid=grid,
            in_specs=[spec for _, spec in ins] + [ANY] * (total + len(onto)),
            out_specs=[spec for _, _, spec in outs],
            scratch_shapes=[pltpu.VMEM(w.shape, BF) for w in weights]
            + list(scratch)
            + ([pltpu.SemaphoreType.DMA((total,))] if total else []),
        ),
        out_shape=[jax.ShapeDtypeStruct(shape, kind) for shape, kind, _ in outs],
        input_output_aliases={1 + len(ins) + total + at: at for at in range(len(onto))},
        compiler_params=pltpu.CompilerParams(vmem_limit_bytes=LIMIT),
        cost_estimate=estimate(cost),
        name=name,
    )(scalars, *[a for a, _ in ins], *[p for w in weights for p in w.arrays], *onto)


COST = 1e6


def estimate(micros):
    return pl.CostEstimate(flops=int(micros * COST), bytes_accessed=1 << 10, transcendentals=0)


def program(shards, ranks):
    ring = shards // 2
    by_line = ring == 4

    def after(value, *others):
        return lax.optimization_barrier((value,) + others)[0] if others else value

    last, leaving = {}, {}

    def send(lane, value, axis, pairs):
        sent = lax.ppermute(after(value, *last.get(lane, ())), axis, pairs)
        last[lane] = (sent,)
        return sent

    def pair(value, lane="pair"):
        return send(lane, value, "fsdp", [(f, f ^ 1) for f in range(shards)])

    def across(value, bits):
        return send(("rank", min(bits, 2)), value, "replica", [(r, r ^ bits) for r in range(ranks)])

    def hop(value, by, sources):
        return send(by, value, "fsdp", [(2 * at + y, 2 * (at + by) + y) for at in sources for y in range(2)])

    def gather(piece, z, y, *ahead):
        got = [(piece, z * 2 + y)]

        def exchange(value, at):
            other = pair(value)
            got.extend([(value, at * 2 + y), (other, at * 2 + (y ^ 1))] if at is not z else [(other, at * 2 + (y ^ 1))])
            return other

        up1, down1 = hop(piece, 1, (0, 1, 2)), hop(piece, -1, (1, 2, 3))
        other = exchange(piece, z)
        up2, down2 = hop(after(up1, other, *ahead), 1, (1, 2)), hop(after(down1, other, *ahead), -1, (1, 2))
        other = exchange(jnp.where(z == 3, up1, down1), jnp.where(z == 3, 2, z + 1))
        up3, down3 = hop(after(up2, other), 1, (2,)), hop(after(down2, other), -1, (1,))
        exchange(jnp.where(z >= 2, up2, down2), (z + 2) % 4)
        far = jnp.where(z == 0, down3, jnp.where(z == 3, up3, up1))
        exchange(far, jnp.where(z == 0, 3, jnp.where(z == 3, 0, z - 1)))
        return got

    def gather_whole(piece):
        return lax.all_gather(piece, "fsdp", axis=0, tiled=True)

    def plus(*terms):
        total = terms[0].astype(F32)
        for term in terms[1:]:
            total = total + term.astype(F32)
        return total.astype(BF)

    def scatter_whole(value):
        return lax.psum_scatter(value, "fsdp", scatter_dimension=0, tiled=True)

    def scatter_along(value):
        lines = [[2 * at + y for at in range(ring)] for y in range(2)]
        flat = value.reshape((-1,) + value.shape[2:])
        return lax.psum_scatter(flat, "fsdp", scatter_dimension=0, tiled=True, axis_index_groups=lines)

    def gather_group(value):
        two = across(value, 2)
        return [value, across(value, 1), two, across(two, 1)]

    def scatter_group(parts):
        leaving["far"] = plus(parts[2], across(parts[3], 1))
        far = across(leaving["far"], 2)
        return parts[0], across(parts[1], 1), far

    def by_rank(pieces, rank):
        low, high = rank % 2 == 1, rank // 2 == 1
        a, b, c, d = pieces
        a, b, c, d = (jnp.where(low, *p) for p in ((b, a), (a, b), (d, c), (c, d)))
        return [jnp.where(high, *p) for p in ((c, a), (d, b), (a, c), (b, d))]

    def on_device(
        tokens, seq_lengths, attn_gain, w_query, w_key, w_value, w_outgate, w_alpha, w_beta, conv_weight,
        decay_log, decay_bias, head_gain, w_output, mlp_gain, w_gate, w_up, w_down, cotangent,
    ):
        rows, model = tokens.shape
        heads = decay_log.shape[0]
        heads_local = heads // ranks
        width = model // ranks
        piece_rows = w_query.shape[0]
        hidden_piece = w_down.shape[0] // ranks
        hidden_cols = shards * hidden_piece
        taps_count = conv_weight.shape[0]
        buffers = ranks
        group = buffers * rows
        rank = lax.axis_index("replica")
        place = lax.axis_index("fsdp")
        z, y = place // 2, place % 2

        def owner(dz, dy):
            return ((z + dz) % ring) * 2 + (y ^ dy)

        own = lambda w: lax.dynamic_slice_in_dim(w, rank * width, width, axis=1)

        conv_parts = conv_weight.shape[1] // piece_rows
        conv_cols = conv_weight.T.reshape(conv_parts, piece_rows, taps_count)
        conv_cols = jnp.swapaxes(conv_cols, 0, 1).reshape(piece_rows, conv_parts * taps_count)
        small = jnp.concatenate([w_alpha, w_beta, attn_gain[:, None], mlp_gain[:, None], conv_cols], axis=1)
        small = jnp.pad(small, ((0, 0), (0, 128 - small.shape[1])))
        shard_in = jnp.concatenate([own(w_query), own(w_key), own(w_value), own(w_outgate), small, own(w_output)], axis=1)
        hidden = lambda w: lax.dynamic_index_in_dim(
            w.reshape(piece_rows, shards, ranks, hidden_piece), rank, 2, keepdims=False
        ).reshape(piece_rows, hidden_cols)
        shard_gu = jnp.concatenate([hidden(w_gate), hidden(w_up)], axis=1)
        shard_d = lax.dynamic_slice_in_dim(w_down, rank * hidden_piece, hidden_piece, axis=0)

        live = (jnp.arange(rows, dtype=jnp.int32) < jnp.sum(seq_lengths[0])).astype(F32)[:, None]
        note = jnp.pad(seq_lengths.astype(BF), ((0, 15), (0, model - seq_lengths.shape[1])))
        tokens_noted = jnp.concatenate([tokens, note], axis=0)
        upstream_own = cotangent * live.astype(BF)

        token_slots = gather_group(tokens_noted)
        whole_in = gather_whole(shard_in)
        upstream_slots = gather_group(upstream_own)
        lengths = jnp.stack([t[rows, : seq_lengths.shape[1]] for t in token_slots]).astype(jnp.int32)
        if by_line:
            got_d = [(piece, f * hidden_piece) for piece, f in gather(shard_d, z, y, token_slots[2])]
        else:
            got_d = [(gather_whole(shard_d), 0)]
        ahead = [*token_slots[1:], *upstream_slots[1:], *[piece for piece, _ in got_d[1:]]]
        whole_gu = gather_whole(after(shard_gu, whole_in, *ahead))

        in_cols = 4 * width + 128
        full_in = Pieces([(whole_in, 0)], model, 0, in_cols)
        full_out = Pieces([(whole_in, 0)], model, in_cols, width)
        full_gu = Pieces([(whole_gu, 0)], model)
        full_down = Pieces(got_d, hidden_cols)

        info = [rank, y]
        by_slot = lambda cols: pl.BlockSpec((rows, cols), lambda i, info: (i ^ info[0], 0))
        by_row = lambda cols: pl.BlockSpec((rows, cols), lambda i, info: (i, 0))
        a_row = pl.BlockSpec((1, 1, rows), lambda i, info: (i, 0, 0))
        lanes_of = lambda info, j: pl.ds(pl.multiple_of((info[0] ^ j) * width, 128), width)
        own_lanes = lambda info: lanes_of(info, 0)
        gain_rows = 16
        split = 2 if by_line else 1
        kept_cols = model // split

        def write_split(info, value_ref, refs):
            if not by_line:
                refs[0][...] = value_ref[...]
                return
            for other, ref in enumerate(refs):
                for at in range(ring):
                    first = (2 * at + (info[1] ^ other)) * piece_rows
                    ref[:, at * piece_rows : (at + 1) * piece_rows] = value_ref[:, pl.ds(pl.multiple_of(first, 128), piece_rows)]


        def enter_body(info, ins, weights, outs, extra):
            (w_ref,) = weights
            x_refs = ins
            pre_ref, x_own_ref, lane_ref = outs[0], outs[1 + split], outs[2 + split]
            x_ref, normed_ref = extra
            step = pl.program_id(0)

            @pl.when(step == 0)
            def _():
                picked = lax.broadcasted_iota(jnp.int32, (gain_rows, 128), 0) + 2 * heads
                picked = (picked == lax.broadcasted_iota(jnp.int32, (gain_rows, 128), 1)).astype(BF)
                for first in range(0, model, 256):
                    block = w_ref[first : first + 256, 4 * width :]
                    lane_ref[:, first : first + 256] = dot(picked, block, NT)

            for j in range(len(x_refs)):
                @pl.when(step == j)
                def _():
                    x_ref[...] = x_refs[j][:rows]

            x_own_ref[...] = x_ref[:, own_lanes(info)]
            x = x_ref[...].astype(F32)
            scale = lax.rsqrt(jnp.mean(x * x, axis=1, keepdims=True) + EPS)
            normed = (x * scale * lane_ref[0:1]).astype(BF)
            normed_ref[...] = normed
            write_split(info, normed_ref, outs[1 : 1 + split])
            pre_ref[...] = dot(normed, w_ref[...])

        slot = pl.BlockSpec((rows, model), lambda i, info: (0, 0))
        entered = []
        for first in (0, 2):
            some = lambda cols: pl.BlockSpec((rows, cols), lambda i, info: ((i + info[2]) ^ info[0], 0))
            entered.append(kernel_call(
                enter_body, "enter", 11, (2,), [rank, y, first],
                [(x, whole(x)) for x in token_slots[first : first + 2]], [full_in],
                [
                    ((group, in_cols), F32, some(in_cols)), *[((group, kept_cols), BF, some(kept_cols))] * split,
                    ((group, width), BF, some(width)),
                    ((gain_rows, model), F32, pl.BlockSpec((gain_rows, model), lambda i, info: (0, 0))),
                ],
                [pltpu.VMEM((rows, model), BF)] * 2, entered[0][: 2 + split] if entered else (),
            ))
        pre, normed, x_cols = entered[1][0], entered[1][1 : 1 + split], entered[1][1 + split]
        lanes = entered[0][2 + split]
        gain_one = lanes[0]
        own_gain = pl.BlockSpec((1, width), lambda i, info: (0, 0))
        gain_two = lax.dynamic_slice_in_dim(lanes[1:2], rank * width, width, axis=1)
        conv_all = lanes[2 : 2 + conv_parts * taps_count].reshape(conv_parts, taps_count, shards, piece_rows)
        conv_all = conv_all.transpose(1, 2, 0, 3).reshape(taps_count, 3, model)
        taps = lax.dynamic_slice_in_dim(conv_all, rank * width, width, axis=2).reshape(taps_count, 3 * width)

        rank_arr = rank[None].astype(jnp.int32)
        made = ()
        for at in range(buffers):
            source = entered[at // 2][0]
            if at == 2:
                source = pre
            made = mixer_forward(
                at, rank_arr, lengths, decay_log, decay_bias, source, taps, head_gain[None], heads_local, made
            )
        gated, inverse = made

        def leave_body(info, ins, weights, outs, extra):
            (w_ref,) = weights
            x_ref, gain_ref = ins[ranks:]
            resid_ref, branch_ref, scaled_ref, square_ref = outs[split:]
            (all_ref,) = extra
            for j in range(ranks):
                all_ref[:, lanes_of(info, j)] = ins[j][...]
            write_split(info, all_ref, outs[:split])
            branch = dot(all_ref[...], w_ref[...])
            resid = x_ref[...].astype(F32) + branch
            resid_ref[...] = resid
            branch_ref[...] = branch
            scaled_ref[...] = (resid * gain_ref[...]).astype(BF)
            square_ref[0] = to_row(jnp.sum(resid * resid, axis=1, keepdims=True), diagonal(rows))

        *gated_all, resid, branch, scaled, square = kernel_call(
            leave_body, "leave", 9, (buffers,), info,
            [(g, by_row(width)) for g in gather_group(gated)] + [(x_cols, by_row(width)), (gain_two, own_gain)],
            [full_out],
            [
                *[((group, kept_cols), BF, by_row(kept_cols))] * split, ((group, width), F32, by_row(width)),
                ((group, width), F32, by_row(width)), ((group, width), BF, by_row(width)),
                ((buffers, 1, rows), F32, a_row),
            ],
            [pltpu.VMEM((rows, model), BF)],
        )
        squares = gather_group(square)

        def inverse_scale(square_refs):
            total = square_refs[0][0]
            for ref in square_refs[1:]:
                total = total + ref[0]
            return lax.rsqrt(to_col(total, diagonal(rows)) / model + EPS)

        def hidden_body(info, ins, weights, outs, extra):
            w_ref, d_ref = weights
            hidden_ref, grad_ref, stat_ref, u_ref, u_own_ref = outs[split:]
            (all_ref,) = extra
            for j in range(ranks):
                @pl.when(pl.program_id(0) ^ info[0] == j)
                def _():
                    u_ref[...] = ins[2 * ranks + j][...]

            u_own_ref[...] = u_ref[:, own_lanes(info)]
            for j in range(ranks):
                all_ref[:, lanes_of(info, j)] = ins[j][...]
            write_split(info, all_ref, outs[:split])
            inv = inverse_scale(ins[ranks : 2 * ranks])
            raw_gate = dot(all_ref[...], w_ref[:, :hidden_cols])
            raw_up = dot(all_ref[...], w_ref[:, hidden_cols:])
            grad_hidden = dot(u_ref[...], d_ref[...], NT)
            gate, up = raw_gate * inv, raw_up * inv
            sig = jax.nn.sigmoid(gate)
            opened = gate * sig
            hidden_ref[...] = (opened * up).astype(BF)
            grad_hidden = grad_hidden * inv
            grad_gate = (grad_hidden * up * (sig * (1.0 + gate * (1.0 - sig)))).astype(BF)
            grad_up = (grad_hidden * opened).astype(BF)
            grad_ref[:, :hidden_cols] = grad_gate
            grad_ref[:, hidden_cols:] = grad_up
            stat = jnp.sum(raw_gate * grad_gate.astype(F32) + raw_up * grad_up.astype(F32), axis=1, keepdims=True)
            stat_ref[0] = to_row(stat, diagonal(rows))

        *scaled_all, hidden_b, grad_gu, stat, upstream, u_cols = kernel_call(
            hidden_body, "hidden", 33, (buffers,), info,
            [(s, by_row(width)) for s in gather_group(scaled)] + [(s, a_row) for s in squares]
            + [(u, slot) for u in upstream_slots],
            [full_gu, full_down],
            [
                *[((group, kept_cols), BF, by_row(kept_cols))] * split, ((group, hidden_cols), BF, by_row(hidden_cols)),
                ((group, 2 * hidden_cols), BF, by_row(2 * hidden_cols)), ((buffers, 1, rows), F32, a_row),
                ((group, model), BF, by_row(model)), ((group, width), BF, by_row(width)),
            ],
            [pltpu.VMEM((rows, model), BF)],
        )
        stats = gather_group(stat)

        def back_body(info, ins, weights, outs, extra):
            for j in range(ranks):
                outs[j][...] = dot(ins[0][...], weights[0][lanes_of(info, j)], NT).astype(BF)

        def scattered(lefts, right, piece, *begin):
            if not by_line:
                value = dot(lefts[0], right, TN).astype(BF)
                return value, lambda *events: (scatter_whole(value), value)
            kept, sent = (dot(left, right, TN).astype(BF) for left in lefts)
            return exchanged(kept, sent, piece, *begin)

        def exchanged(kept, sent, piece, *begin):
            given = lax.ppermute(after(sent, *begin), "fsdp", [(f, f ^ 1) for f in range(shards)])

            def end(*events):
                total = plus(after(kept, *events), given)
                return scatter_along(total.reshape(ring, piece, -1)), total

            return sent, end

        sent_gate, end_gate = scattered(scaled_all, grad_gu[:, :hidden_cols], piece_rows)
        parts = kernel_call(
            back_body, "back", 19, (buffers,), info, [(after(grad_gu, sent_gate), by_row(2 * hidden_cols))], [full_gu],
            [((group, width), BF, by_row(width))] * ranks,
        )
        terms_two = scatter_group(parts)

        sent_up, end_up = scattered(scaled_all, grad_gu[:, hidden_cols:], piece_rows, parts[0])
        d_down = dot(hidden_b, upstream, TN).astype(BF)

        def turn_body(info, ins, weights, outs, extra):
            (w_ref,) = weights
            own_ref, near_ref, far_ref, resid_ref, u_ref, gain_ref = ins[:6]
            grad_ref, out_refs, gain_out_ref = outs[0], outs[1 : 1 + ranks], outs[1 + ranks]

            @pl.when(pl.program_id(0) == 0)
            def _():
                gain_out_ref[...] = jnp.zeros_like(gain_out_ref)

            grad_two = own_ref[...].astype(F32) + near_ref[...].astype(F32) + far_ref[...].astype(F32)
            resid = resid_ref[...]
            inv = inverse_scale(ins[6 : 6 + ranks])
            total = ins[6 + ranks][0]
            for ref in ins[7 + ranks :]:
                total = total + ref[0]
            stat = to_col(total, diagonal(rows))
            gain_out_ref[...] += jnp.sum(grad_two * resid, axis=0, keepdims=True)
            grad = u_ref[...].astype(F32) + gain_ref[...] * grad_two - resid * (inv * inv * stat / model)
            grad = grad.astype(BF)
            grad_ref[...] = grad
            for j in range(ranks):
                out_refs[j][...] = dot(grad, w_ref[lanes_of(info, j)], NT).astype(BF)

        turned = kernel_call(
            turn_body, "turn", 9, (buffers,), info,
            [(t, by_row(width)) for t in terms_two]
            + [(after(resid, d_down, sent_up), by_row(width)), (u_cols, by_row(width)), (gain_two, own_gain)]
            + [(s, a_row) for s in squares] + [(s, a_row) for s in stats],
            [full_out],
            [((group, width), BF, by_row(width))] * (1 + ranks) + [((1, width), F32, own_gain)],
        )
        grad_branch, grad_mlp_gain = turned[0], turned[1 + ranks][0]
        terms_gated = scatter_group(turned[1 : 1 + ranks])
        if by_line:
            placed = d_down.reshape(ring, 2, hidden_piece, model)
            side = lambda at: lax.dynamic_index_in_dim(placed, at, 1, keepdims=False).reshape(ring * hidden_piece, model)
            _, end_down = exchanged(side(y), side(1 - y), hidden_piece, grad_branch)
        else:
            end_down = lambda *events: (scatter_whole(d_down), d_down)
        own_block = lambda value, j: lax.dynamic_slice_in_dim(value, (rank ^ j) * rows, rows, axis=0)

        def to_tokens(value):
            pieces = [own_block(value, 0)] + [across(own_block(value, j), j) for j in range(1, ranks)]
            return jnp.concatenate(by_rank(pieces, rank), axis=1).astype(F32)

        def down_body(info, ins, weights, outs, extra):
            (full,) = extra
            full[...] = dot(ins[0][...], weights[0][...])
            full[:, own_lanes(info)] += ins[1][...]
            for j in range(ranks):
                @pl.when(pl.program_id(0) == j)
                def _():
                    outs[j][...] = full[...].astype(BF)

        down = kernel_call(
            down_body, "down", 14, (ranks,), info, [(after(hidden_b, leaving["far"]), by_slot(hidden_cols)), (branch, by_slot(width))], [full_down],
            [((rows, model), BF, slot)] * ranks, [pltpu.VMEM((rows, model), F32)],
        )
        down_terms = scatter_group(down)
        output = tokens.astype(F32)
        for term in down_terms:
            output = output + term.astype(F32)
        output = (output * live).astype(BF)
        grad_resid_own = to_tokens(grad_branch)

        made = ()
        share_gate, _ = end_gate(down[0])
        ahead = [tuple(down), (), (), (down_terms[2],)]
        for at in range(buffers):
            made = mixer_backward(
                at, rank_arr, lengths, decay_log, decay_bias, after(pre, *ahead[at]), taps, head_gain[None], inverse,
                terms_gated, heads_local, made,
            )
            if at == 0:
                _, end_out = scattered(gated_all, grad_branch, piece_rows, made[1])
            if at == 1:
                share_up, _ = end_up(made[1])
        d_pre, d_taps, d_head_gain, d_decay = made
        cuts = ((0, 2 * width), (2 * width, 2 * width + 128))
        ends_in = [scattered(normed, d_pre[:, first : first + count], piece_rows) for first, count in cuts]
        d_in = [sent for sent, _ in ends_in]
        share_d, _ = end_down(*d_in)

        def first_body(info, ins, weights, outs, extra):
            result = dot(ins[0][...], weights[0][...], NT).astype(BF)
            for j in range(ranks):
                @pl.when(pl.program_id(0) == j)
                def _():
                    outs[j][...] = result

        grad_slots = kernel_call(
            first_body, "first", 19, (ranks,), info, [(after(d_pre, *d_in), by_slot(in_cols))], [full_in],
            [((rows, model), BF, slot)] * ranks,
        )
        gate_slots = gather_group(share_gate)
        first_terms = scatter_group(grad_slots)
        grad_one = sum(t.astype(F32) for t in first_terms)
        share_o, sum_o = end_out(grad_slots[0])
        share_a, sum_a = ends_in[0][1](sum_o, first_terms[2])
        share_b, sum_b = ends_in[1][1](sum_a)
        x_own = tokens.astype(F32)
        inv_one = lax.rsqrt(jnp.mean(x_own * x_own, axis=-1, keepdims=True) + EPS)
        grad_attn_gain = jnp.sum(grad_one * x_own * inv_one, axis=0)
        pulled = gain_one * grad_one
        grad_x = inv_one * pulled - x_own * (inv_one**3 * jnp.mean(pulled * x_own, axis=-1, keepdims=True))
        grad_tokens = (grad_resid_own + grad_x).astype(BF)

        def finish_body(info, ins, weights, outs, extra):
            for j in range(ranks):
                for at, out in enumerate(outs):
                    out[:, lanes_of(info, j)] = ins[j][:, at * width : (at + 1) * width].astype(F32)

        def finish(slots, count):
            tile = piece_rows // 4
            tiled = lambda cols: pl.BlockSpec((tile, cols), lambda i, info: (i, 0))
            return kernel_call(
                finish_body, "finish", 5, (4,), info, [(v, tiled(v.shape[1])) for v in slots], [],
                [((piece_rows, model), F32, tiled(model))] * count,
            )

        def unhide_body(info, ins, weights, outs, extra):
            (held,) = extra
            for j in range(ranks):
                held[info[0] ^ j] = ins[j][...]
            for out in outs:
                for f in range(shards):
                    first = f * hidden_piece
                    out[:, f * ranks * hidden_piece : (f + 1) * ranks * hidden_piece] = jnp.concatenate(
                        [held[b, :, first : first + hidden_piece].astype(F32) for b in range(ranks)], axis=1
                    )

        def unhide(slots):
            tile = piece_rows // 4
            tiled = lambda cols: pl.BlockSpec((tile, cols), lambda i, info: (i, 0))
            full = shards * ranks * hidden_piece
            [result] = kernel_call(
                unhide_body, "unhide", 8, (4,), info, [(v, tiled(v.shape[1])) for v in slots], [],
                [((piece_rows, full), F32, tiled(full))], [pltpu.VMEM((ranks, tile, hidden_cols), BF)],
            )
            return result

        own_cols = lambda value: lax.dynamic_update_slice_in_dim(
            jnp.zeros(value.shape[:-1] + (model,), F32), value, rank * width, axis=value.ndim - 1
        )
        packed = jnp.concatenate(
            [
                own_cols(d_taps.reshape(taps_count, 3, width)).reshape(-1),
                own_cols(grad_mlp_gain),
                grad_attn_gain,
                d_head_gain[0],
                d_decay[0, :heads],
                d_decay[1, :heads],
            ]
        )
        total = jnp.pad(packed, (0, -packed.size % 1024)).reshape(-1, 128)
        for bits in (1, 2):
            total = total + lax.ppermute(total, "replica", [(r, r ^ bits) for r in range(ranks)])
        bits = 1
        while bits < shards:
            total = total + lax.ppermute(total, "fsdp", [(f, f ^ bits) for f in range(shards)])
            bits *= 2
        total = total.reshape(-1)
        conv_size = taps_count * 3 * model
        sum_conv = total[:conv_size].reshape(taps_count, shards, -1)
        sum_conv = lax.dynamic_index_in_dim(sum_conv, place, 1, keepdims=False)
        at = conv_size
        sum_mlp_gain = lax.dynamic_slice_in_dim(total, at + place * piece_rows, piece_rows)
        sum_attn_gain = lax.dynamic_slice_in_dim(total, at + model + place * piece_rows, piece_rows)
        at += 2 * model
        sum_head_gain = total[at : at + head_gain.size]
        at += head_gain.size
        sum_log, sum_bias = total[at : at + heads], total[at + heads : at + 2 * heads]

        up_slots = gather_group(share_up)
        out_gate = unhide(gate_slots)
        d_slots = gather_group(after(share_d, out_gate))
        out_up = unhide(up_slots)
        o_slots = gather_group(after(share_o, out_up))
        out_down = jnp.concatenate(by_rank(d_slots, rank), axis=0).astype(F32)
        a_slots = gather_group(after(share_a, out_down))
        [out_output] = finish(o_slots, 1)
        out_query, out_key = finish(a_slots, 2)
        finished = (out_gate, out_up, out_down, out_output, output, grad_tokens, sum_conv, out_query, out_key)
        share_b, *finished = lax.optimization_barrier((share_b, *finished))
        out_gate, out_up, out_down, out_output, output, grad_tokens, sum_conv, out_query, out_key = finished
        b_slots = gather_group(share_b)
        out_value, out_outgate = finish(b_slots, 2)
        low = [p[:, 2 * width :].astype(F32) for p in b_slots]
        low = (low[0] + low[1]) + (low[2] + low[3])
        out_alpha, out_beta = low[:, :heads], low[:, heads : 2 * heads]
        return (
            output, grad_tokens, sum_attn_gain, out_query, out_key, out_value, out_outgate, out_alpha, out_beta,
            sum_conv, sum_log, sum_bias, sum_head_gain, out_output, sum_mlp_gain, out_gate, out_up, out_down,
        )

    return on_device


def solution(mesh):
    rows, cols = P("fsdp", None), P("fsdp")
    tokens = P(("replica", "fsdp"), None)
    return jax.shard_map(
        program(mesh.shape["fsdp"], mesh.shape["replica"]),
        mesh=mesh,
        in_specs=(
            tokens, tokens, cols, rows, rows, rows, rows, rows, rows, P(None, "fsdp"), P(), P(), P(), rows, cols,
            rows, rows, rows, tokens,
        ),
        out_specs=(
            tokens, tokens, cols, rows, rows, rows, rows, rows, rows, P(None, "fsdp"), P(), P(), P(), rows, cols,
            rows, rows, rows,
        ),
        check_vma=False,
    )
```
